32 devices in a mesh: dp: 16 (over z, x, core), tensor: 2 (over y).
Axes of the slice: x: 2, y: 2, z: 4, core: 2. Of those that a mesh axis runs over, the one named last changes fastest.
Arguments:
- hidden_in: bfloat16 [32768, 768], P('dp'), may hold values from -6 to 6
- query_weight: bfloat16 [768, 768], P(None, 'tensor'), may hold values from -0.3125 to 0.3125
- key_weight: bfloat16 [768, 768], P(None, 'tensor'), may hold values from -0.3125 to 0.3125
- value_weight: bfloat16 [768, 768], P(None, 'tensor'), may hold values from -0.21875 to 0.21875
- query_bias: bfloat16 [768], P('tensor'), may hold values from -3 to 3
- value_bias: bfloat16 [768], P('tensor'), may hold values from -3 to 3
- mixer_weight: bfloat16 [768, 768], P('tensor'), may hold values from -1.25 to 1.25
- mixer_bias: bfloat16 [768], replicated, may hold values from -3 to 3
- first_gain: bfloat16 [768], replicated, may hold values from 0.5 to 1.5
- first_bias: bfloat16 [768], replicated, may hold values from -3 to 3
- inner_weight: bfloat16 [768, 3072], P(None, 'tensor'), may hold values from -0.21875 to 0.21875
- inner_bias: bfloat16 [3072], P('tensor'), may hold values from -3 to 3
- outer_weight: bfloat16 [3072, 768], P('tensor'), may hold values from -0.109375 to 0.109375
- outer_bias: bfloat16 [768], replicated, may hold values from -3 to 3
- second_gain: bfloat16 [768], replicated, may hold values from 0.5 to 1.5
- second_bias: bfloat16 [768], replicated, may hold values from -3 to 3
- lengths: int32 [64, 4], P('dp'), may hold values from 33 to 512, as said below
- cotangent: bfloat16 [32768, 768], P('dp'), may hold values from -6 to 6
Outputs:
- layer_out: bfloat16 [32768, 768], P('dp')
- input_grad: bfloat16 [32768, 768], P('dp')
- query_weight_grad: float32 [768, 768], P(None, 'tensor')
- key_weight_grad: float32 [768, 768], P(None, 'tensor')
- value_weight_grad: float32 [768, 768], P(None, 'tensor')
- query_bias_grad: float32 [768], P('tensor')
- value_bias_grad: float32 [768], P('tensor')
- mixer_weight_grad: float32 [768, 768], P('tensor')
- mixer_bias_grad: float32 [768], replicated
- first_gain_grad: float32 [768], replicated
- first_bias_grad: float32 [768], replicated
- inner_weight_grad: float32 [768, 3072], P(None, 'tensor')
- inner_bias_grad: float32 [3072], P('tensor')
- outer_weight_grad: float32 [3072, 768], P('tensor')
- outer_bias_grad: float32 [768], replicated
- second_gain_grad: float32 [768], replicated
- second_bias_grad: float32 [768], replicated
The draws below stay inside these ranges and needn't reach their ends.
Inputs may be any that keep to these rules, and one draw needn't show every extreme that they name: lengths[b, j] counts the live tokens of the j-th sequence of block b, whose sequences have 512 / 2**((b % 4) % 3) positions each; no entry exceeds its sequence's positions; entries with j at or past the block's number of sequences are not read; some sequence is full.
All inputs are finite; a program needn't handle non-finite values.
Results may differ from the reference program's by a relative error of at most 0.014.
The reference program's roundings to bfloat16 on the way count: a program that leaves them out, or rounds other values in their place, can miss the bound.
Values sent between devices are 32-bit elements; how exact they have to be, the bound alone decides.
No kernel may reach another device: no remote copies, remote signals or barrier semaphores. Data moves between devices by JAX's collectives and lax.ppermute only.
A program may use at most 256 MiB of HBM per device.

```python
import jax
import jax.numpy as jnp
from jax import lax

D = 768
HEADS = 12
FF = 3072
HD = 64
MAXLEN = 512
BLOCKS_DEV = 4
TOK_DEV = 2048
BLOCKS = 64
TOKENS = 32768
N_DP = 16


def draw_lengths(key, part):
    key = jax.random.fold_in(key, 7)
    key_level, key_bits, key_pick = jax.random.split(key, 3)
    row_count = N_DP * BLOCKS_DEV
    row_index = jnp.arange(row_count, dtype=jnp.int32)
    block_kind = row_index % BLOCKS_DEV % 3
    seq_span = jnp.right_shift(jnp.int32(MAXLEN), block_kind)
    fill_level = jax.random.randint(key_level, (N_DP,), 4, 9)
    upper_bound = jnp.maximum(1, seq_span * fill_level[row_index // BLOCKS_DEV] // 8)
    random_bits = jax.random.randint(key_bits, (row_count, 4), 0, 1 << 20)
    lengths = upper_bound[:, None] - random_bits % ((upper_bound[:, None] + 1) // 2)
    chosen = jax.random.randint(key_pick, (), 0, N_DP)
    lengths = lengths.at[chosen * BLOCKS_DEV, 0].set(MAXLEN)
    return lengths.astype(jnp.int32)


def block_levels(stream_key, shape, cuts, low, largest):
    def one(dim, parts):
        draws = jax.random.uniform(jax.random.fold_in(jax.random.fold_in(stream_key, 6), dim), (parts,), jnp.float32, low / len(cuts), largest / len(cuts))
        return jnp.repeat(jnp.exp(draws), shape[dim] // parts).reshape((-1,) + (1,) * (len(shape) - dim - 1))

    level = one(*cuts[0])
    for cut in cuts[1:]:
        level = level * one(*cut)
    return level


def normal_values(rng, shape, spread, limit, pieces=(), kind=jnp.bfloat16):
    values = spread * jax.random.normal(rng, shape, jnp.float32)
    if pieces:
        values = values * block_levels(rng, shape, pieces, -0.22, 0.18)
    return jnp.clip(values, -limit, limit).astype(kind)


def setup_inputs(seed: int = 0) -> dict:
    key_list = jax.random.split(jax.random.key(seed), 19)
    hidden_in = normal_values(key_list[0], (TOKENS, D), 1.0, 6.0, ((0, 16),))
    query_weight = normal_values(key_list[1], (D, D), (D // 2) ** -0.5, 0.3125, ((1, 2),))
    key_weight = normal_values(key_list[2], (D, D), (D // 2) ** -0.5, 0.3125, ((1, 2),))
    value_weight = normal_values(key_list[3], (D, D), D ** -0.5, 0.21875, ((1, 2),))
    query_bias = normal_values(key_list[4], (D,), 0.5, 3.0, ((0, 2),))
    value_bias = normal_values(key_list[5], (D,), 0.5, 3.0, ((0, 2),))
    mixer_weight = normal_values(key_list[6], (D, D), (D * 16 // MAXLEN) ** -0.5, 1.25, ((0, 2),))
    mixer_bias = normal_values(key_list[7], (D,), 0.5, 3.0)
    first_gain = jnp.clip(1.0 + 0.1 * jax.random.normal(key_list[8], (D,), jnp.float32), 0.5, 1.5).astype(jnp.bfloat16)
    first_bias = normal_values(key_list[9], (D,), 0.5, 3.0)
    inner_weight = normal_values(key_list[10], (D, FF), D ** -0.5, 0.21875, ((1, 2),))
    inner_bias = normal_values(key_list[11], (FF,), 0.5, 3.0, ((0, 2),))
    outer_weight = normal_values(key_list[12], (FF, D), FF ** -0.5, 0.109375, ((0, 2),))
    outer_bias = normal_values(key_list[13], (D,), 0.5, 3.0)
    second_gain = jnp.clip(1.0 + 0.1 * jax.random.normal(key_list[14], (D,), jnp.float32), 0.5, 1.5).astype(jnp.bfloat16)
    second_bias = normal_values(key_list[15], (D,), 0.5, 3.0)
    lengths = draw_lengths(jax.random.fold_in(key_list[18], 71), 0)
    cotangent = normal_values(key_list[17], (TOKENS, D), 1.0, 6.0, ((0, 16),))
    return {"hidden_in": hidden_in, "query_weight": query_weight, "key_weight": key_weight, "value_weight": value_weight, "query_bias": query_bias, "value_bias": value_bias, "mixer_weight": mixer_weight, "mixer_bias": mixer_bias, "first_gain": first_gain, "first_bias": first_bias, "inner_weight": inner_weight, "inner_bias": inner_bias, "outer_weight": outer_weight, "outer_bias": outer_bias, "second_gain": second_gain, "second_bias": second_bias, "lengths": lengths, "cotangent": cotangent}


EPSILON = 1e-06

@jax.custom_vjp
def low(v):
    return lax.optimization_barrier(v.astype(jnp.bfloat16)).astype(jnp.float32)

@jax.custom_vjp
def low_back(v):
    return v

def low_keep(v):
    return (low(v), None)

def low_pass(kept, grad):
    return (grad,)

def back_keep(v):
    return (v, None)

def back_low(kept, grad):
    return (low(grad),)
low.defvjp(low_keep, low_pass)
low_back.defvjp(back_keep, back_low)

def matmul(left, right):
    return jnp.dot(left, right, precision=lax.Precision.HIGHEST)

def block_masks(lengths_block, block_kind):
    seq_span = jnp.right_shift(jnp.int32(MAXLEN), block_kind)
    position = jnp.arange(MAXLEN, dtype=jnp.int32)
    segment = position // seq_span
    offset = position - segment * seq_span
    slot_index = jnp.arange(4, dtype=jnp.int32)
    picked = lax.optimization_barrier(jnp.sum(jnp.where(segment[:, None] == slot_index[None, :], lengths_block[None, :], 0), axis=1))
    live_rows = offset < picked
    allowed = (segment[:, None] == segment[None, :]) & live_rows[None, :]
    return (allowed, live_rows)

def normalize(values, norm_gain, norm_bias):
    center = values - lax.optimization_barrier(jnp.mean(values, axis=-1, keepdims=True))
    inverse = lax.rsqrt(lax.optimization_barrier(jnp.mean(center * center, axis=-1, keepdims=True)) + EPSILON)
    return center * inverse * norm_gain + norm_bias

def attend(query, keys, values, allowed):
    query_heads = query.reshape(MAXLEN, HEADS, HD)
    key_heads = keys.reshape(MAXLEN, HEADS, HD)
    value_heads = values.reshape(MAXLEN, HEADS, HD)
    scores = jnp.einsum('qhd,khd->hqk', query_heads, key_heads, precision=lax.Precision.HIGHEST) * HD ** (-0.5)
    scores = low_back(scores)
    scores = jnp.where(allowed[None, :, :], scores, -1e+30)
    probs = low(jax.nn.softmax(scores, axis=-1))
    context = jnp.einsum('hqk,khd->qhd', probs, value_heads, precision=lax.Precision.HIGHEST)
    return context.reshape(MAXLEN, D)

def group_forward(params, tokens, allowed):
    query_weight, key_weight, value_weight, query_bias, value_bias, mixer_weight, mixer_bias, first_gain, first_bias, inner_weight, inner_bias, outer_weight, outer_bias, second_gain, second_bias = params
    query = low(low_back(matmul(tokens, query_weight) + query_bias))
    keys = low(low_back(matmul(tokens, key_weight)))
    values = low(low_back(matmul(tokens, value_weight) + value_bias))
    context = jax.vmap(attend)(query.reshape(BLOCKS_DEV, MAXLEN, D), keys.reshape(BLOCKS_DEV, MAXLEN, D), values.reshape(BLOCKS_DEV, MAXLEN, D), allowed)
    context = low(low_back(context.reshape(TOK_DEV, D)))
    mixed = low_back(matmul(context, mixer_weight)) + mixer_bias
    first = normalize(tokens + mixed, first_gain, first_bias)
    inner = low_back(matmul(low(first), inner_weight) + inner_bias)
    active = low(jax.nn.gelu(inner, approximate=False))
    outer = low_back(matmul(active, outer_weight)) + outer_bias
    return normalize(first + outer, second_gain, second_bias)

def reference(hidden_in, query_weight, key_weight, value_weight, query_bias, value_bias, mixer_weight, mixer_bias, first_gain, first_bias, inner_weight, inner_bias, outer_weight, outer_bias, second_gain, second_bias, lengths, cotangent):
    block_kinds = jnp.arange(BLOCKS, dtype=jnp.int32) % BLOCKS_DEV % 3
    allowed, live_rows = jax.vmap(block_masks)(lengths, block_kinds)
    params = tuple((weight.astype(jnp.float32) for weight in (query_weight, key_weight, value_weight, query_bias, value_bias, mixer_weight, mixer_bias, first_gain, first_bias, inner_weight, inner_bias, outer_weight, outer_bias, second_gain, second_bias)))
    tokens = hidden_in.astype(jnp.float32)
    grouped_masks = allowed.reshape(N_DP, BLOCKS_DEV, MAXLEN, MAXLEN)

    def forward(weights, inputs):

        def one_group(group_pair):
            return group_forward(weights, group_pair[0], group_pair[1])
        outputs = lax.map(jax.checkpoint(one_group), (inputs.reshape(N_DP, TOK_DEV, D), grouped_masks))
        return outputs.reshape(TOKENS, D)
    result, pullback = jax.vjp(forward, params, tokens)
    grad_out = cotangent.astype(jnp.float32) * live_rows.reshape(TOKENS, 1).astype(jnp.float32)
    param_grads, token_grad = pullback(grad_out)
    query_weight_grad, key_weight_grad, value_weight_grad, query_bias_grad, value_bias_grad, mixer_weight_grad, mixer_bias_grad, first_gain_grad, first_bias_grad, inner_weight_grad, inner_bias_grad, outer_weight_grad, outer_bias_grad, second_gain_grad, second_bias_grad = param_grads
    return (result.astype(jnp.bfloat16), token_grad.astype(jnp.bfloat16), query_weight_grad, key_weight_grad, value_weight_grad, query_bias_grad, value_bias_grad, mixer_weight_grad, mixer_bias_grad, first_gain_grad, first_bias_grad, inner_weight_grad, inner_bias_grad, outer_weight_grad, outer_bias_grad, second_gain_grad, second_bias_grad)
```

```python
import math
from functools import partial

import jax
import jax.numpy as jnp
from jax import lax
from jax.experimental import pallas as pl
from jax.experimental.pallas import tpu as pltpu
from jax.sharding import PartitionSpec as P

HD = 64
MAXLEN = 512
EPSILON = 1e-06
INV_SQRT2 = 1.0 / math.sqrt(2.0)
INV_SQRT_2PI = 1.0 / math.sqrt(2.0 * math.pi)
NEG = -1e30
BF = jnp.bfloat16
F32 = jnp.float32
VMEM_LIMIT = 56 * 1024 * 1024
V_QV, V_MB, V_FG, V_FB, V_IB, V_OB, V_SG, V_SB, V_ROWS = 0, 1, 2, 3, 4, 6, 7, 8, 16


def dot(a, b):
    return lax.dot_general(a, b, (((1,), (0,)), ((), ())), preferred_element_type=F32)


def dot_bt(a, b):
    return lax.dot_general(a, b, (((1,), (1,)), ((), ())), preferred_element_type=F32)


def dot_at(a, b):
    return lax.dot_general(a, b, (((0,), (0,)), ((), ())), preferred_element_type=F32)


def head_lanes(rows):
    return lax.broadcasted_iota(jnp.int32, (rows, 2 * HD), 1) < HD


def params(**kw):
    return pltpu.CompilerParams(vmem_limit_bytes=VMEM_LIMIT, **kw)


def full(shape):
    return pl.BlockSpec(shape, lambda b: (0,) * len(shape), pipeline_mode=pl.Buffered(1))


def rows_spec(cols, rows=MAXLEN):
    return pl.BlockSpec((rows, cols), lambda b: (b, 0))


SMEM = pl.BlockSpec(memory_space=pltpu.SMEM)


def attn_fwd_kernel(len_ref, h_ref, wq_ref, wk_ref, wv_ref, vec_ref, q_ref, k_ref, v_ref, c_ref, l_ref):
    half = wq_ref.shape[1]
    pairs = half // (2 * HD)
    b = pl.program_id(0)
    h = h_ref[...]
    q_ref[...] = (dot(h, wq_ref[...]) + vec_ref[V_QV : V_QV + 1, :half]).astype(BF)
    k_ref[...] = dot(h, wk_ref[...]).astype(BF)
    v_ref[...] = (dot(h, wv_ref[...]) + vec_ref[V_QV : V_QV + 1, half:]).astype(BF)
    l_ref[...] = jnp.zeros_like(l_ref)
    for kind in range(3):

        @pl.when(lax.rem(b, 3) == kind)
        def _():
            span = MAXLEN >> kind
            for seq in range(1 << kind):
                rows = slice(seq * span, (seq + 1) * span)
                live = lax.broadcasted_iota(jnp.int32, (1, span), 1) < len_ref[b, seq]
                bias = jnp.where(live, 0.0, NEG)
                low_lanes = head_lanes(span)
                logs = jnp.zeros((span, 128), F32)
                lane = lax.broadcasted_iota(jnp.int32, (span, 128), 1)
                for pair in range(pairs):
                    cols = slice(pair * 2 * HD, (pair + 1) * 2 * HD)
                    qp = q_ref[rows, cols] * BF(0.125)
                    kp = k_ref[rows, cols]
                    vp = v_ref[rows, cols]
                    outs = []
                    for sub in range(2):
                        qh = jnp.where(low_lanes if sub == 0 else ~low_lanes, qp, BF(0))
                        s = dot_bt(qh, kp) + bias
                        m = jnp.max(s, axis=-1, keepdims=True)
                        e = jnp.exp(s - m)
                        z = jnp.sum(e, axis=-1, keepdims=True)
                        p = (e * (1.0 / z)).astype(BF)
                        logs = jnp.where(lane == 2 * pair + sub, m + jnp.log(z), logs)
                        outs.append(dot(p, vp))
                    c_ref[rows, cols] = jnp.where(low_lanes, outs[0], outs[1]).astype(BF)
                l_ref[:, rows] = logs.T[:8]


def attn_fwd(lengths, hidden, wq, wk, wv, vec):
    n, d = hidden.shape
    half = wq.shape[1]
    blocks = n // MAXLEN
    wide = jax.ShapeDtypeStruct((n, half), BF)
    return pl.pallas_call(
        attn_fwd_kernel,
        grid=(blocks,),
        in_specs=[SMEM, rows_spec(d), full((d, half)), full((d, half)), full((d, half)), full(vec.shape)],
        out_specs=[rows_spec(half)] * 4 + [pl.BlockSpec((8, MAXLEN), lambda b: (b, 0))],
        out_shape=[wide] * 4 + [jax.ShapeDtypeStruct((8 * blocks, MAXLEN), F32)],
        compiler_params=params(),
        cost_estimate=pl.CostEstimate(flops=12_000_000_000, bytes_accessed=16_000_000, transcendentals=0),
        name="attn_fwd",
    )(lengths, hidden, wq, wk, wv, vec)


def live_column(len_ref, b):
    pos = lax.broadcasted_iota(jnp.int32, (MAXLEN, 1), 0)
    kind = lax.rem(b, 3)
    shift = 9 - kind
    seg = lax.shift_right_logical(pos, shift)
    off = pos - lax.shift_left(seg, shift)
    picked = jnp.full((MAXLEN, 1), len_ref[b, 0], jnp.int32)
    for slot in range(1, 4):
        picked = jnp.where(seg == slot, len_ref[b, slot], picked)
    return (off < picked).astype(F32)


def norm_stats(x):
    center = x - jnp.mean(x, axis=-1, keepdims=True)
    inverse = lax.rsqrt(jnp.mean(center * center, axis=-1, keepdims=True) + EPSILON)
    return center * inverse, inverse


def accumulate(ref, value, first_step):
    @pl.when(first_step)
    def _():
        ref[...] = value

    @pl.when(jnp.logical_not(first_step))
    def _():
        ref[...] += value


def ff_fwd_kernel(
    len_ref, h_ref, co_ref, cp_ref, cot_ref, wmo_ref, wmp_ref, wio_ref, wip_ref, woo_ref, wop_ref, vec_ref, pvec_ref,
    out_ref, x_ref, low_ref, gs_ref, lo_ref, gpo_ref, gpp_ref, owg_ref, sums_ref, act_ref, pa_ref, pb_ref,
):
    b = pl.program_id(0)
    d = h_ref.shape[1]
    ff = wio_ref.shape[1]
    width = 512
    pa_ref[...] = dot(co_ref[...], wmo_ref[...])
    pb_ref[...] = dot(cp_ref[...], wmp_ref[...])
    mixed = (pa_ref[...] + pb_ref[...]) + vec_ref[V_MB : V_MB + 1, :]
    x = h_ref[...].astype(F32) + mixed
    x_ref[...] = x
    n1, _ = norm_stats(x)
    first = n1 * vec_ref[V_FG : V_FG + 1, :] + vec_ref[V_FB : V_FB + 1, :]
    low = first.astype(BF)
    low_ref[...] = low
    for wi, wo, vec, gp_ref, part_ref, keep in (
        (wio_ref, woo_ref, vec_ref, gpo_ref, pa_ref, True),
        (wip_ref, wop_ref, pvec_ref, gpp_ref, pb_ref, False),
    ):
        part = None
        for c in range(ff // width):
            cols = slice(c * width, (c + 1) * width)
            row, at = divmod(c * width, d)
            if at + width <= d:
                bias = vec[V_IB + row : V_IB + row + 1, at : at + width]
            else:
                bias = jnp.concatenate(
                    [vec[V_IB + row : V_IB + row + 1, at:], vec[V_IB + row + 1 : V_IB + row + 2, : at + width - d]], axis=1
                )
            inner = dot(low, wi[:, cols]) + bias
            cdf = 0.5 * (1.0 + lax.erf(inner * INV_SQRT2))
            gp_ref[:, cols] = cdf + inner * (jnp.exp(-0.5 * inner * inner) * INV_SQRT_2PI)
            active = (inner * cdf).astype(BF)
            if keep:
                act_ref[:, cols] = active
            term = dot(active, wo[cols, :])
            part = term if part is None else part + term
        part_ref[...] = part
    r = first + ((pa_ref[...] + pb_ref[...]) + vec_ref[V_OB : V_OB + 1, :])
    n2, inv2 = norm_stats(r)
    gain = vec_ref[V_SG : V_SG + 1, :]
    out_ref[...] = (n2 * gain + vec_ref[V_SB : V_SB + 1, :]).astype(BF)
    g = cot_ref[...].astype(F32) * live_column(len_ref, b)
    scaled = g * gain
    gs = inv2 * (
        scaled - jnp.mean(scaled, axis=-1, keepdims=True) - n2 * jnp.mean(scaled * n2, axis=-1, keepdims=True)
    )
    gs_ref[...] = gs
    lo = gs.astype(BF)
    lo_ref[...] = lo
    sums = jnp.concatenate(
        [
            jnp.sum(gs, axis=0, keepdims=True),
            jnp.sum(g * n2, axis=0, keepdims=True),
            jnp.sum(g, axis=0, keepdims=True),
            jnp.zeros((5, d), F32),
        ],
        axis=0,
    )
    accumulate(sums_ref, sums, b == 0)
    accumulate(owg_ref, dot_at(act_ref[...], lo), b == 0)


def ff_fwd(lengths, hidden, co, cp, cot, wmo, wmp, wio, wip, woo, wop, vec, pvec):
    n, d = hidden.shape
    half = co.shape[1]
    ff = wio.shape[1]
    return pl.pallas_call(
        ff_fwd_kernel,
        grid=(n // MAXLEN,),
        in_specs=[
            SMEM, rows_spec(d), rows_spec(half), rows_spec(half), rows_spec(d), full((half, d)), full((half, d)),
            full((d, ff)), full((d, ff)), full((ff, d)), full((ff, d)), full(vec.shape), full(pvec.shape),
        ],
        out_specs=[
            rows_spec(d), rows_spec(d), rows_spec(d), rows_spec(d), rows_spec(d), rows_spec(ff), rows_spec(ff),
            full((ff, d)), full((8, d)),
        ],
        out_shape=[
            jax.ShapeDtypeStruct((n, d), BF),
            jax.ShapeDtypeStruct((n, d), F32),
            jax.ShapeDtypeStruct((n, d), BF),
            jax.ShapeDtypeStruct((n, d), F32),
            jax.ShapeDtypeStruct((n, d), BF),
            jax.ShapeDtypeStruct((n, ff), F32),
            jax.ShapeDtypeStruct((n, ff), F32),
            jax.ShapeDtypeStruct((ff, d), F32),
            jax.ShapeDtypeStruct((8, d), F32),
        ],
        scratch_shapes=[pltpu.VMEM((MAXLEN, ff), BF), pltpu.VMEM((MAXLEN, d), F32), pltpu.VMEM((MAXLEN, d), F32)],
        compiler_params=params(),
        cost_estimate=pl.CostEstimate(flops=30_000_000_000, bytes_accessed=70_000_000, transcendentals=0),
        name="ff_fwd",
    )(lengths, hidden, co, cp, cot, wmo, wmp, wio, wip, woo, wop, vec, pvec)


def ff_bwd_kernel(
    lo_ref, gs_ref, x_ref, low_ref, gpo_ref, gpp_ref, co_ref, wio_ref, wip_ref, woo_ref, wop_ref, vec_ref,
    gm_ref, lm_ref, iwg_ref, mwg_ref, sums_ref, isum_ref, gi_ref, pa_ref, pb_ref,
):
    b = pl.program_id(0)
    d = lo_ref.shape[1]
    ff = wio_ref.shape[1]
    width = 512
    lo = lo_ref[...]
    for wi, wo, gp_ref, part_ref, keep in (
        (wio_ref, woo_ref, gpo_ref, pa_ref, True),
        (wip_ref, wop_ref, gpp_ref, pb_ref, False),
    ):
        part = None
        for c in range(ff // width):
            cols = slice(c * width, (c + 1) * width)
            gi32 = dot_bt(lo, wo[cols, :]) * gp_ref[:, cols]
            gi = gi32.astype(BF)
            if keep:
                gi_ref[:, cols] = gi
            term = dot_bt(gi, wi[:, cols])
            part = term if part is None else part + term
        part_ref[...] = part
    gi = gi_ref[...]
    accumulate(iwg_ref, dot_at(low_ref[...], gi), b == 0)
    accumulate(isum_ref, jnp.sum(gi.astype(F32), axis=0, keepdims=True), b == 0)
    g = gs_ref[...] + (pa_ref[...] + pb_ref[...])
    n1, inv1 = norm_stats(x_ref[...])
    scaled = g * vec_ref[V_FG : V_FG + 1, :]
    gm = inv1 * (
        scaled - jnp.mean(scaled, axis=-1, keepdims=True) - n1 * jnp.mean(scaled * n1, axis=-1, keepdims=True)
    )
    gm_ref[...] = gm
    lm = gm.astype(BF)
    lm_ref[...] = lm
    sums = jnp.concatenate(
        [
            jnp.sum(gm, axis=0, keepdims=True),
            jnp.sum(g * n1, axis=0, keepdims=True),
            jnp.sum(g, axis=0, keepdims=True),
            jnp.zeros((5, d), F32),
        ],
        axis=0,
    )
    accumulate(sums_ref, sums, b == 0)
    accumulate(mwg_ref, dot_at(co_ref[...], lm), b == 0)


def ff_bwd(lo, gs, x, low, gpo, gpp, co, wio, wip, woo, wop, vec):
    n, d = lo.shape
    half = co.shape[1]
    ff = wio.shape[1]
    return pl.pallas_call(
        ff_bwd_kernel,
        grid=(n // MAXLEN,),
        in_specs=[
            rows_spec(d), rows_spec(d), rows_spec(d), rows_spec(d), rows_spec(ff), rows_spec(ff), rows_spec(half),
            full((d, ff)), full((d, ff)), full((ff, d)), full((ff, d)), full(vec.shape),
        ],
        out_specs=[rows_spec(d), rows_spec(d), full((d, ff)), full((half, d)), full((8, d)), full((1, ff))],
        out_shape=[
            jax.ShapeDtypeStruct((n, d), F32),
            jax.ShapeDtypeStruct((n, d), BF),
            jax.ShapeDtypeStruct((d, ff), F32),
            jax.ShapeDtypeStruct((half, d), F32),
            jax.ShapeDtypeStruct((8, d), F32),
            jax.ShapeDtypeStruct((1, ff), F32),
        ],
        scratch_shapes=[pltpu.VMEM((MAXLEN, ff), BF), pltpu.VMEM((MAXLEN, d), F32), pltpu.VMEM((MAXLEN, d), F32)],
        compiler_params=params(),
        cost_estimate=pl.CostEstimate(flops=26_000_000_000, bytes_accessed=60_000_000, transcendentals=0),
        name="ff_bwd",
    )(lo, gs, x, low, gpo, gpp, co, wio, wip, woo, wop, vec)


def attn_bwd_kernel(own, len_ref, lm_ref, wm_ref, q_ref, k_ref, v_ref, l_ref, wq_ref, wk_ref, wv_ref, *rest):
    if own:
        h_ref, part_ref, wg_ref, sums_ref, gc_ref, dq_ref, dk_ref, dv_ref = rest
    else:
        gm_ref, opart_ref, ig_ref, gc_ref, dq_ref, dk_ref, dv_ref, part_ref = rest
    half = wq_ref.shape[1]
    pairs = half // (2 * HD)
    b = pl.program_id(0)
    gc_ref[...] = dot_bt(lm_ref[...], wm_ref[...]).astype(BF)
    for kind in range(3):

        @pl.when(lax.rem(b, 3) == kind)
        def _():
            span = MAXLEN >> kind
            low_lanes = head_lanes(span)
            for seq in range(1 << kind):
                rows = slice(seq * span, (seq + 1) * span)
                live = lax.broadcasted_iota(jnp.int32, (span, 1), 0) < len_ref[b, seq]
                bias = jnp.where(live, 0.0, NEG)
                for pair in range(pairs):
                    cols = slice(pair * 2 * HD, (pair + 1) * 2 * HD)
                    qp = q_ref[rows, cols] * BF(0.125)
                    kp = k_ref[rows, cols]
                    vp = v_ref[rows, cols]
                    up = gc_ref[rows, cols]
                    dqs, dks, dvs = [], [], []
                    for sub in range(2):
                        mask = low_lanes if sub == 0 else ~low_lanes
                        s = dot_bt(kp, jnp.where(mask, qp, BF(0))) + bias
                        p = jnp.exp(s - l_ref[2 * pair + sub : 2 * pair + sub + 1, rows])
                        dp = dot_bt(vp, jnp.where(mask, up, BF(0)))
                        delta = jnp.sum(p * dp, axis=0, keepdims=True)
                        ds = (p * (dp - delta)).astype(BF)
                        dvs.append(dot(p.astype(BF), up))
                        dks.append(dot(ds, qp))
                        dqs.append(dot_at(ds, kp))
                    dv_ref[rows, cols] = jnp.where(low_lanes, dvs[0], dvs[1]).astype(BF)
                    dk_ref[rows, cols] = jnp.where(low_lanes, dks[0], dks[1]).astype(BF)
                    dq_ref[rows, cols] = (jnp.where(low_lanes, dqs[0], dqs[1]) * 0.125).astype(BF)

    dq, dk, dv = dq_ref[...], dk_ref[...], dv_ref[...]
    part = (dot_bt(dq, wq_ref[...]) + dot_bt(dk, wk_ref[...])) + dot_bt(dv, wv_ref[...])
    part_ref[...] = part
    if own:
        sums = jnp.concatenate(
            [jnp.sum(dq.astype(F32), axis=0, keepdims=True), jnp.sum(dv.astype(F32), axis=0, keepdims=True)], axis=1
        )
        accumulate(sums_ref, sums, b == 0)
        h = h_ref[...]
        accumulate(wg_ref, jnp.concatenate([dot_at(h, dq), dot_at(h, dk), dot_at(h, dv)], axis=1), b == 0)
    else:
        ig_ref[...] = (gm_ref[...] + (opart_ref[...] + part_ref[...])).astype(BF)


def attn_bwd(own, lengths, lm, wm, q, k, v, logs, wq, wk, wv, *extra):
    n, d = lm.shape
    half = wq.shape[1]
    if own:
        extra_specs = [rows_spec(d)]
        out_specs = [rows_spec(d), full((d, 3 * half)), full((1, 2 * half))]
        out_shape = [
            jax.ShapeDtypeStruct((n, d), F32),
            jax.ShapeDtypeStruct((d, 3 * half), F32),
            jax.ShapeDtypeStruct((1, 2 * half), F32),
        ]
    else:
        extra_specs = [rows_spec(d), rows_spec(d)]
        out_specs = rows_spec(d)
        out_shape = jax.ShapeDtypeStruct((n, d), BF)
    return pl.pallas_call(
        partial(attn_bwd_kernel, own),
        grid=(n // MAXLEN,),
        in_specs=[
            SMEM, rows_spec(d), full((half, d)), rows_spec(half), rows_spec(half), rows_spec(half),
            pl.BlockSpec((8, MAXLEN), lambda b: (b, 0)), full((d, half)), full((d, half)), full((d, half)), *extra_specs,
        ],
        out_specs=out_specs,
        out_shape=out_shape,
        scratch_shapes=[pltpu.VMEM((MAXLEN, half), BF)] * 4 + ([] if own else [pltpu.VMEM((MAXLEN, d), F32)]),
        compiler_params=params(),
        cost_estimate=pl.CostEstimate(flops=25_000_000_000, bytes_accessed=25_000_000, transcendentals=0),
        name="attn_bwd_own" if own else "attn_bwd_peer",
    )(lengths, lm, wm, q, k, v, logs, wq, wk, wv, *extra)


def cast_kernel(*refs):
    count = len(refs) // 2
    for src, dst in zip(refs[:count], refs[count:]):
        dst[...] = src[...].astype(BF)


def cast_down(arrays):
    return pl.pallas_call(
        cast_kernel,
        out_shape=[jax.ShapeDtypeStruct(a.shape, BF) for a in arrays],
        compiler_params=params(),
        name="cast_down",
    )(*arrays)


def fetch_peer(weights, n_dp):
    me = lax.axis_index("dp")
    got = []
    for w in weights:
        rows = w.shape[0] // n_dp
        piece = lax.dynamic_slice_in_dim(w, me * rows, rows, 0).astype(F32)
        piece = lax.ppermute(piece, "tensor", [(0, 1), (1, 0)])
        got.append(lax.all_gather(piece, "dp", tiled=True))
    return cast_down(got)


def local(
    n_dp, hidden_in, query_weight, key_weight, value_weight, query_bias, value_bias, mixer_weight, mixer_bias,
    first_gain, first_bias, inner_weight, inner_bias, outer_weight, outer_bias, second_gain, second_bias, lengths,
    cotangent,
):
    n, d = hidden_in.shape
    half = query_weight.shape[1]
    ff = inner_weight.shape[1]
    vec = jnp.concatenate(
        [
            query_bias, value_bias, mixer_bias, first_gain, first_bias, inner_bias, outer_bias, second_gain, second_bias,
            jnp.zeros(((V_ROWS - 9) * d,), BF),
        ]
    ).astype(F32).reshape(V_ROWS, d)
    pvec = lax.ppermute(vec, "tensor", [(0, 1), (1, 0)])
    wqp, wkp, wvp, wmp, wip, wop = fetch_peer(
        (query_weight, key_weight, value_weight, mixer_weight, inner_weight, outer_weight), n_dp
    )
    qo, ko, vo, co, lgo = attn_fwd(lengths, hidden_in, query_weight, key_weight, value_weight, vec)
    qp, kp, vp, cp, lgp = attn_fwd(lengths, hidden_in, wqp, wkp, wvp, pvec)
    layer_out, x, low, gs, lo, gpo, gpp, owg, osums = ff_fwd(
        lengths, hidden_in, co, cp, cotangent, mixer_weight, wmp, inner_weight, wip, outer_weight, wop, vec, pvec
    )
    gm, lm, iwg, mwg, isums, ibg = ff_bwd(lo, gs, x, low, gpo, gpp, co, inner_weight, wip, outer_weight, wop, vec)
    part, qkvg, qvsum = attn_bwd(
        True, lengths, lm, mixer_weight, qo, ko, vo, lgo, query_weight, key_weight, value_weight, hidden_in
    )
    input_grad = attn_bwd(False, lengths, lm, wmp, qp, kp, vp, lgp, wqp, wkp, wvp, gm, part)
    small = jnp.concatenate([qvsum.reshape(1, d), isums[:3], osums[:3], ibg.reshape(-1, d)], axis=0)
    owg = lax.psum(owg, "dp")
    iwg = lax.psum(iwg, "dp")
    mwg, qkvg, small = lax.psum((mwg, qkvg, small), "dp")
    return (
        layer_out, input_grad, qkvg[:, :half], qkvg[:, half : 2 * half], qkvg[:, 2 * half :], small[0, :half],
        small[0, half:], mwg, small[1], small[2], small[3], iwg, small[7:].reshape(ff), owg, small[4], small[5],
        small[6],
    )


def solution(mesh):
    col, row, rep = P(None, "tensor"), P("tensor", None), P()
    vec, tok = P("tensor"), P("dp", None)
    return jax.shard_map(
        partial(local, mesh.shape["dp"]),
        mesh=mesh,
        in_specs=(tok, col, col, col, vec, vec, row, rep, rep, rep, col, vec, row, rep, rep, rep, tok, tok),
        out_specs=(tok, tok, col, col, col, vec, vec, row, rep, rep, rep, col, vec, row, rep, rep, rep),
        check_vma=False,
    )
```

```python
import math
from functools import partial

import jax
import jax.numpy as jnp
from jax import lax
from jax.experimental import pallas as pl
from jax.experimental.pallas import tpu as pltpu
from jax.sharding import PartitionSpec as P

HD = 64
MAXLEN = 512
EPSILON = 1e-06
INV_SQRT2 = 1.0 / math.sqrt(2.0)
INV_SQRT_2PI = 1.0 / math.sqrt(2.0 * math.pi)
NEG = -1e30
BF = jnp.bfloat16
F32 = jnp.float32
VMEM_LIMIT = 56 * 1024 * 1024
PAD = 64
V_QV, V_MB, V_FG, V_FB, V_IB, V_OB, V_SG, V_SB, V_ROWS = 0, 1, 2, 3, 4, 6, 7, 8, 16


def dot(a, b):
    return lax.dot_general(a, b, (((1,), (0,)), ((), ())), preferred_element_type=F32)


def dot_bt(a, b):
    return lax.dot_general(a, b, (((1,), (1,)), ((), ())), preferred_element_type=F32)


def dot_at(a, b):
    return lax.dot_general(a, b, (((0,), (0,)), ((), ())), preferred_element_type=F32)


def head_lanes(rows):
    return lax.broadcasted_iota(jnp.int32, (rows, 2 * HD), 1) < HD


def params(**kw):
    return pltpu.CompilerParams(vmem_limit_bytes=VMEM_LIMIT, **kw)


def full(shape):
    return pl.BlockSpec(shape, lambda b: (0,) * len(shape), pipeline_mode=pl.Buffered(1))


def rows_spec(cols, start=0):
    return pl.BlockSpec((MAXLEN, cols), lambda b: (b + start, 0))


SMEM = pl.BlockSpec(memory_space=pltpu.SMEM)
ANY = pl.BlockSpec(memory_space=pl.ANY)
COST = pl.CostEstimate(flops=1_000_000_000, bytes_accessed=1_000_000, transcendentals=0)


def attn_fwd_kernel(start, skip, len_ref, h_ref, wq_ref, wk_ref, wv_ref, vec_ref, *rest):
    q_ref, k_ref, v_ref, c_ref, l_ref = rest[skip:]
    half = wq_ref.shape[1]
    pairs = half // (2 * HD)
    b = pl.program_id(0) + start
    h = h_ref[...]
    q_ref[...] = (dot(h, wq_ref[...]) + vec_ref[V_QV : V_QV + 1, :half]).astype(BF)
    k_ref[...] = dot(h, wk_ref[...]).astype(BF)
    v_ref[...] = (dot(h, wv_ref[...]) + vec_ref[V_QV : V_QV + 1, half:]).astype(BF)
    l_ref[...] = jnp.zeros_like(l_ref)
    for kind in range(3):

        @pl.when(lax.rem(b, 3) == kind)
        def _():
            span = MAXLEN >> kind
            for seq in range(1 << kind):
                rows = slice(seq * span, (seq + 1) * span)
                live = lax.broadcasted_iota(jnp.int32, (1, span), 1) < len_ref[b, seq]
                bias = jnp.where(live, 0.0, NEG)
                low_lanes = head_lanes(span)
                logs = jnp.zeros((span, 128), F32)
                lane = lax.broadcasted_iota(jnp.int32, (span, 128), 1)
                for pair in range(pairs):
                    cols = slice(pair * 2 * HD, (pair + 1) * 2 * HD)
                    qp = q_ref[rows, cols] * BF(0.125)
                    kp = k_ref[rows, cols]
                    vp = v_ref[rows, cols]
                    outs = []
                    for sub in range(2):
                        qh = jnp.where(low_lanes if sub == 0 else ~low_lanes, qp, BF(0))
                        s = dot_bt(qh, kp) + bias
                        m = jnp.max(s, axis=-1, keepdims=True)
                        e = jnp.exp(s - m)
                        z = jnp.sum(e, axis=-1, keepdims=True)
                        p = (e * (1.0 / z)).astype(BF)
                        logs = jnp.where(lane == 2 * pair + sub, m + jnp.log(z), logs)
                        outs.append(dot(p, vp))
                    c_ref[rows, cols] = jnp.where(low_lanes, outs[0], outs[1]).astype(BF)
                l_ref[:, rows] = logs.T[:8]


def attn_fwd(lengths, hidden, wq, wk, wv, vec, start, count, prior=None, after=()):
    n, d = hidden.shape
    half = wq.shape[1]
    blocks = n // MAXLEN
    wide = jax.ShapeDtypeStruct((n, half), BF)
    prior = list(prior or ())
    extra = prior + list(after)
    return pl.pallas_call(
        partial(attn_fwd_kernel, start, len(extra)),
        grid=(count,),
        in_specs=[
            SMEM, rows_spec(d, start), full((d, half)), full((d, half)), full((d, half)), full(vec.shape),
            *[ANY] * len(extra),
        ],
        out_specs=[rows_spec(half, start)] * 4 + [pl.BlockSpec((8, MAXLEN), lambda b: (b + start, 0))],
        out_shape=[wide] * 4 + [jax.ShapeDtypeStruct((8 * blocks, MAXLEN), F32)],
        input_output_aliases={6 + i: i for i in range(len(prior))},
        compiler_params=params(),
        cost_estimate=COST,
        name="attn_fwd",
    )(lengths, hidden, wq, wk, wv, vec, *extra)


def live_column(len_ref, b):
    pos = lax.broadcasted_iota(jnp.int32, (MAXLEN, 1), 0)
    kind = lax.rem(b, 3)
    shift = 9 - kind
    seg = lax.shift_right_logical(pos, shift)
    off = pos - lax.shift_left(seg, shift)
    picked = jnp.full((MAXLEN, 1), len_ref[b, 0], jnp.int32)
    for slot in range(1, 4):
        picked = jnp.where(seg == slot, len_ref[b, slot], picked)
    return (off < picked).astype(F32)


def norm_stats(x):
    center = x - jnp.mean(x, axis=-1, keepdims=True)
    inverse = lax.rsqrt(jnp.mean(center * center, axis=-1, keepdims=True) + EPSILON)
    return center * inverse, inverse


def accumulate(ref, value, first_step):
    @pl.when(first_step)
    def _():
        ref[...] = value

    @pl.when(jnp.logical_not(first_step))
    def _():
        ref[...] += value


def ff_fwd_kernel(
    len_ref, h_ref, co_ref, cp_ref, cot_ref, wmo_ref, wmp_ref, wio_ref, wip_ref, woo_ref, wop_ref, vec_ref, pvec_ref,
    out_ref, x_ref, low_ref, gs_ref, lo_ref, gpo_ref, gpp_ref, owg_ref, sums_ref, act_ref, pa_ref, pb_ref,
):
    b = pl.program_id(0)
    d = h_ref.shape[1]
    ff = wio_ref.shape[1]
    width = 512
    pa_ref[...] = dot(co_ref[...], wmo_ref[...])
    pb_ref[...] = dot(cp_ref[...], wmp_ref[...])
    mixed = (pa_ref[...] + pb_ref[...]) + vec_ref[V_MB : V_MB + 1, :]
    x = h_ref[...].astype(F32) + mixed
    x_ref[...] = x
    n1, _ = norm_stats(x)
    first = n1 * vec_ref[V_FG : V_FG + 1, :] + vec_ref[V_FB : V_FB + 1, :]
    low = first.astype(BF)
    low_ref[...] = low
    for wi, wo, vec, gp_ref, part_ref, keep in (
        (wio_ref, woo_ref, vec_ref, gpo_ref, pa_ref, True),
        (wip_ref, wop_ref, pvec_ref, gpp_ref, pb_ref, False),
    ):
        part = None
        for c in range(ff // width):
            cols = slice(c * width, (c + 1) * width)
            row, at = divmod(c * width, d)
            if at + width <= d:
                bias = vec[V_IB + row : V_IB + row + 1, at : at + width]
            else:
                bias = jnp.concatenate(
                    [vec[V_IB + row : V_IB + row + 1, at:], vec[V_IB + row + 1 : V_IB + row + 2, : at + width - d]], axis=1
                )
            inner = dot(low, wi[:, cols]) + bias
            cdf = 0.5 * (1.0 + lax.erf(inner * INV_SQRT2))
            gp_ref[:, cols] = cdf + inner * (jnp.exp(-0.5 * inner * inner) * INV_SQRT_2PI)
            active = (inner * cdf).astype(BF)
            if keep:
                act_ref[:, cols] = active
            term = dot(active, wo[cols, :])
            part = term if part is None else part + term
        part_ref[...] = part
    r = first + ((pa_ref[...] + pb_ref[...]) + vec_ref[V_OB : V_OB + 1, :])
    n2, inv2 = norm_stats(r)
    gain = vec_ref[V_SG : V_SG + 1, :]
    out_ref[...] = (n2 * gain + vec_ref[V_SB : V_SB + 1, :]).astype(BF)
    g = cot_ref[...].astype(F32) * live_column(len_ref, b)
    scaled = g * gain
    gs = inv2 * (
        scaled - jnp.mean(scaled, axis=-1, keepdims=True) - n2 * jnp.mean(scaled * n2, axis=-1, keepdims=True)
    )
    gs_ref[...] = gs
    lo = gs.astype(BF)
    lo_ref[...] = lo
    sums = jnp.concatenate(
        [
            jnp.sum(gs, axis=0, keepdims=True),
            jnp.sum(g * n2, axis=0, keepdims=True),
            jnp.sum(g, axis=0, keepdims=True),
            jnp.zeros((5, d), F32),
        ],
        axis=0,
    )
    accumulate(sums_ref, sums, b == 0)
    accumulate(owg_ref, dot_at(act_ref[...], lo), b == 0)


def ff_fwd(lengths, hidden, co, cp, cot, wmo, wmp, wio, wip, woo, wop, vec, pvec):
    n, d = hidden.shape
    half = co.shape[1]
    ff = wio.shape[1]
    return pl.pallas_call(
        ff_fwd_kernel,
        grid=(n // MAXLEN,),
        in_specs=[
            SMEM, rows_spec(d), rows_spec(half), rows_spec(half), rows_spec(d), full((half, d)), full((half, d)),
            full((d, ff)), full((d, ff)), full((ff, d)), full((ff, d)), full(vec.shape), full(pvec.shape),
        ],
        out_specs=[
            rows_spec(d), rows_spec(d), rows_spec(d), rows_spec(d), rows_spec(d), rows_spec(ff), rows_spec(ff),
            full((ff, d)), full((8, d)),
        ],
        out_shape=[
            jax.ShapeDtypeStruct((n, d), BF),
            jax.ShapeDtypeStruct((n, d), F32),
            jax.ShapeDtypeStruct((n, d), BF),
            jax.ShapeDtypeStruct((n, d), F32),
            jax.ShapeDtypeStruct((n, d), BF),
            jax.ShapeDtypeStruct((n, ff), F32),
            jax.ShapeDtypeStruct((n, ff), F32),
            jax.ShapeDtypeStruct((ff, d), F32),
            jax.ShapeDtypeStruct((8, d), F32),
        ],
        scratch_shapes=[pltpu.VMEM((MAXLEN, ff), BF), pltpu.VMEM((MAXLEN, d), F32), pltpu.VMEM((MAXLEN, d), F32)],
        compiler_params=params(),
        cost_estimate=COST,
        name="ff_fwd",
    )(lengths, hidden, co, cp, cot, wmo, wmp, wio, wip, woo, wop, vec, pvec)


def ff_bwd_half(lo, wi_ref, wo_ref, gp_ref, gi_ref, part_ref):
    width = 512
    part = None
    for c in range(wi_ref.shape[1] // width):
        cols = slice(c * width, (c + 1) * width)
        gi = (dot_bt(lo, wo_ref[cols, :]) * gp_ref[:, cols]).astype(BF)
        if gi_ref is not None:
            gi_ref[:, cols] = gi
        term = dot_bt(gi, wi_ref[:, cols])
        part = term if part is None else part + term
    part_ref[...] = part


def ff_bwd_own_kernel(lo_ref, low_ref, gp_ref, wi_ref, wo_ref, part_ref, iwg_ref, isum_ref, gi_ref):
    b = pl.program_id(0)
    ff_bwd_half(lo_ref[...], wi_ref, wo_ref, gp_ref, gi_ref, part_ref)
    gi = gi_ref[...]
    accumulate(iwg_ref, dot_at(low_ref[...], gi), b == 0)
    accumulate(isum_ref, jnp.sum(gi.astype(F32), axis=0, keepdims=True), b == 0)


def ff_bwd_own(lo, low, gp, wi, wo):
    n, d = lo.shape
    ff = wi.shape[1]
    return pl.pallas_call(
        ff_bwd_own_kernel,
        grid=(n // MAXLEN,),
        in_specs=[rows_spec(d), rows_spec(d), rows_spec(ff), full((d, ff)), full((ff, d))],
        out_specs=[rows_spec(d), full((d, ff)), full((1, ff))],
        out_shape=[
            jax.ShapeDtypeStruct((n, d), F32),
            jax.ShapeDtypeStruct((d, ff), F32),
            jax.ShapeDtypeStruct((1, ff), F32),
        ],
        scratch_shapes=[pltpu.VMEM((MAXLEN, ff), BF)],
        compiler_params=params(),
        cost_estimate=COST,
        name="ff_bwd_own",
    )(lo, low, gp, wi, wo)


def ff_bwd_peer_kernel(
    skip, lo_ref, gs_ref, x_ref, gp_ref, opart_ref, co_ref, wi_ref, wo_ref, vec_ref, *rest
):
    gm_ref, lm_ref, mwg_ref, sums_ref, part_ref = rest[skip:]
    b = pl.program_id(0)
    d = lo_ref.shape[1]
    ff_bwd_half(lo_ref[...], wi_ref, wo_ref, gp_ref, None, part_ref)
    g = gs_ref[...] + (opart_ref[...] + part_ref[...])
    n1, inv1 = norm_stats(x_ref[...])
    scaled = g * vec_ref[V_FG : V_FG + 1, :]
    gm = inv1 * (
        scaled - jnp.mean(scaled, axis=-1, keepdims=True) - n1 * jnp.mean(scaled * n1, axis=-1, keepdims=True)
    )
    gm_ref[...] = gm
    lm = gm.astype(BF)
    lm_ref[...] = lm
    sums = jnp.concatenate(
        [
            jnp.sum(gm, axis=0, keepdims=True),
            jnp.sum(g * n1, axis=0, keepdims=True),
            jnp.sum(g, axis=0, keepdims=True),
            jnp.zeros((5, d), F32),
        ],
        axis=0,
    )
    accumulate(sums_ref, sums, b == 0)
    accumulate(mwg_ref, dot_at(co_ref[...], lm), b == 0)


def ff_bwd_peer(lo, gs, x, gp, opart, co, wi, wo, vec, *after):
    n, d = lo.shape
    half = co.shape[1]
    ff = wi.shape[1]
    return pl.pallas_call(
        partial(ff_bwd_peer_kernel, len(after)),
        grid=(n // MAXLEN,),
        in_specs=[
            rows_spec(d), rows_spec(d), rows_spec(d), rows_spec(ff), rows_spec(d), rows_spec(half), full((d, ff)),
            full((ff, d)), full(vec.shape), *[ANY] * len(after),
        ],
        out_specs=[rows_spec(d), rows_spec(d), full((half, d)), full((8, d))],
        out_shape=[
            jax.ShapeDtypeStruct((n, d), F32),
            jax.ShapeDtypeStruct((n, d), BF),
            jax.ShapeDtypeStruct((half, d), F32),
            jax.ShapeDtypeStruct((8, d), F32),
        ],
        scratch_shapes=[pltpu.VMEM((MAXLEN, d), F32)],
        compiler_params=params(),
        cost_estimate=COST,
        name="ff_bwd_peer",
    )(lo, gs, x, gp, opart, co, wi, wo, vec, *after)


def attn_bwd_kernel(own, start, skip, len_ref, lm_ref, wm_ref, q_ref, k_ref, v_ref, l_ref, wq_ref, wk_ref, wv_ref, *rest):
    if own:
        h_ref, *given = rest[: 2 if start else 5]
        rest = rest[2 if start else 5 :][skip:]
        part_ref, wg_ref, gc_ref, dq_ref, dk_ref, dv_ref = rest
    else:
        gm_ref, opart_ref = rest[:2]
        ig_ref, gc_ref, dq_ref, dk_ref, dv_ref, part_ref = rest[2 + skip :]
    half = wq_ref.shape[1]
    pairs = half // (2 * HD)
    b = pl.program_id(0) + start
    gc_ref[...] = dot_bt(lm_ref[...], wm_ref[...]).astype(BF)
    for kind in range(3):

        @pl.when(lax.rem(b, 3) == kind)
        def _():
            span = MAXLEN >> kind
            low_lanes = head_lanes(span)
            for seq in range(1 << kind):
                rows = slice(seq * span, (seq + 1) * span)
                live = lax.broadcasted_iota(jnp.int32, (span, 1), 0) < len_ref[b, seq]
                bias = jnp.where(live, 0.0, NEG)
                for pair in range(pairs):
                    cols = slice(pair * 2 * HD, (pair + 1) * 2 * HD)
                    qp = q_ref[rows, cols] * BF(0.125)
                    kp = k_ref[rows, cols]
                    vp = v_ref[rows, cols]
                    up = gc_ref[rows, cols]
                    dqs, dks, dvs = [], [], []
                    for sub in range(2):
                        mask = low_lanes if sub == 0 else ~low_lanes
                        s = dot_bt(kp, jnp.where(mask, qp, BF(0))) + bias
                        p = jnp.exp(s - l_ref[2 * pair + sub : 2 * pair + sub + 1, rows])
                        dp = dot_bt(vp, jnp.where(mask, up, BF(0)))
                        delta = jnp.sum(p * dp, axis=0, keepdims=True)
                        ds = (p * (dp - delta)).astype(BF)
                        dvs.append(dot(p.astype(BF), up))
                        dks.append(dot(ds, qp))
                        dqs.append(dot_at(ds, kp))
                    dv_ref[rows, cols] = jnp.where(low_lanes, dvs[0], dvs[1]).astype(BF)
                    dk_ref[rows, cols] = jnp.where(low_lanes, dks[0], dks[1]).astype(BF)
                    dq_ref[rows, cols] = (jnp.where(low_lanes, dqs[0], dqs[1]) * 0.125).astype(BF)

    dq, dk, dv = dq_ref[...], dk_ref[...], dv_ref[...]
    part = (dot_bt(dq, wq_ref[...]) + dot_bt(dk, wk_ref[...])) + dot_bt(dv, wv_ref[...])
    part_ref[...] = part
    if own:
        d = h_ref.shape[1]
        sums = jnp.concatenate(
            [jnp.sum(dq.astype(F32), axis=0, keepdims=True), jnp.sum(dv.astype(F32), axis=0, keepdims=True)], axis=1
        )
        h = h_ref[...]
        first_step = b == start

        @pl.when(first_step)
        def _():
            if start:
                wg_ref[...] = given[0][...]
                return
            mwg_ref, fsum_ref, isum_ref, osum_ref = given
            wg_ref[:d, 3 * half :] = jnp.concatenate([mwg_ref[:, :half], mwg_ref[:, half:]], axis=0)
            pad = jnp.zeros((1, d), F32)
            top = jnp.concatenate([pad, fsum_ref[0:1, :]], axis=1)
            mid = jnp.concatenate([fsum_ref[1:2, :], fsum_ref[2:3, :]], axis=1)
            low = jnp.concatenate([osum_ref[0:1, :], osum_ref[1:2, :]], axis=1)
            end = jnp.concatenate([osum_ref[2:3, :], pad], axis=1)
            wg_ref[d : d + 8, :] = jnp.concatenate(
                [top, mid, isum_ref[...], low, end, jnp.zeros((3, 2 * d), F32)], axis=0
            )
            wg_ref[d + 8 :, :] = jnp.zeros((wg_ref.shape[0] - d - 8, 2 * d), F32)

        for i, grad in enumerate((dq, dk, dv)):
            value = dot_at(h, grad)
            cols = slice(i * half, (i + 1) * half)

            if start:
                wg_ref[:d, cols] += value
                continue

            @pl.when(first_step)
            def _(value=value, cols=cols):
                wg_ref[:d, cols] = value

            @pl.when(jnp.logical_not(first_step))
            def _(value=value, cols=cols):
                wg_ref[:d, cols] += value

        wg_ref[d : d + 1, :d] += sums
    else:
        ig_ref[...] = (gm_ref[...] + (opart_ref[...] + part_ref[...])).astype(BF)


def attn_bwd(own, start, count, lengths, lm, wm, q, k, v, logs, wq, wk, wv, extra, prior=None, after=()):
    n, d = lm.shape
    half = wq.shape[1]
    after = ([] if prior is None else [prior]) + list(after)
    if own:
        extra_specs = [rows_spec(d, start)] + [full(x.shape) for x in extra[1:]]
        out_specs = [rows_spec(d, start), full((d + PAD, 4 * half))]
        out_shape = [jax.ShapeDtypeStruct((n, d), F32), jax.ShapeDtypeStruct((d + PAD, 4 * half), F32)]
    else:
        extra_specs = [rows_spec(d, start)] * 2
        out_specs = [rows_spec(d, start)]
        out_shape = [jax.ShapeDtypeStruct((n, d), BF)]
    return pl.pallas_call(
        partial(attn_bwd_kernel, own, start, len(after)),
        grid=(count,),
        in_specs=[
            SMEM, rows_spec(d, start), full((half, d)), rows_spec(half, start), rows_spec(half, start),
            rows_spec(half, start), pl.BlockSpec((8, MAXLEN), lambda b: (b + start, 0)), full((d, half)),
            full((d, half)), full((d, half)), *extra_specs, *[ANY] * len(after),
        ],
        out_specs=out_specs,
        out_shape=out_shape,
        input_output_aliases={} if prior is None else {10 + len(extra): 0},
        scratch_shapes=[pltpu.VMEM((MAXLEN, half), BF)] * 4 + ([] if own else [pltpu.VMEM((MAXLEN, d), F32)]),
        compiler_params=params(),
        cost_estimate=COST,
        name="attn_bwd_own" if own else "attn_bwd_peer",
    )(lengths, lm, wm, q, k, v, logs, wq, wk, wv, *extra, *after)


CORE, NEAR, FAR = 1, 2, 4
TENSOR_SWAP = [(0, 1), (1, 0)]


def bit_of(mask):
    return (lax.axis_index("dp") & mask) != 0


def swap(x, mask, n_dp):
    return lax.ppermute(x, "dp", [(i, i ^ mask) for i in range(n_dp)])


def in_order(mask, mine, other):
    return jnp.where(bit_of(mask), jnp.concatenate([other, mine]), jnp.concatenate([mine, other]))


def away(x, mask):
    rows = x.shape[0] // 2
    return lax.dynamic_slice_in_dim(x, jnp.where(bit_of(mask), 0, rows), rows, 0)


def kept(x, mask):
    rows = x.shape[0] // 2
    return lax.dynamic_slice_in_dim(x, jnp.where(bit_of(mask), rows, 0), rows, 0)


def beyond(x, n_dp):
    mask = 4 * FAR
    while mask < n_dp:
        x = x + swap(x, mask, n_dp)
        mask *= 2
    return x


def piece(arrays, masks, base, rows):
    index = jnp.int32(0)
    for mask in masks:
        index = index * 2 + bit_of(mask).astype(jnp.int32)
    cut = [lax.dynamic_slice_in_dim(a, base + index * rows, rows, 0) for a in arrays]
    return jnp.concatenate(cut, axis=1).astype(F32)


def tie(*arrays):
    return lax.optimization_barrier(arrays)


def assemble_kernel(square, a_ref, ra_ref, b_ref, rb_ref, *outs):
    rows = a_ref.shape[0]
    odd = lax.axis_index("dp") & CORE
    for base, mine, other in ((0, a_ref, ra_ref), (2 * rows, b_ref, rb_ref)):
        for ref, side in ((mine, odd), (other, 1 - odd)):
            at = pl.ds(pl.multiple_of(base + side * rows, 16), rows)
            if not square:
                outs[0][at, :] = ref[...].astype(BF)
                continue
            half = ref.shape[1] // 4
            for i in range(3):
                outs[i][at, :] = ref[:, i * half : (i + 1) * half].astype(BF)
            at = pl.ds(pl.multiple_of(side * rows, 16), rows)
            left = base == 0
            cols = slice(0, half) if left else slice(half, 2 * half)
            outs[3][at, cols] = ref[:, 3 * half :].astype(BF)


def assemble(square, a, ra, b, rb):
    rows, cols = 4 * a.shape[0], a.shape[1]
    half = cols // 4
    if square:
        shapes = [(rows, half)] * 3 + [(rows // 2, 2 * half)]
    else:
        shapes = [(rows, cols)]
    return pl.pallas_call(
        partial(assemble_kernel, square),
        out_shape=[jax.ShapeDtypeStruct(shape, BF) for shape in shapes],
        compiler_params=params(),
        cost_estimate=COST,
        name="assemble",
    )(a, ra, b, rb)


def local(
    n_dp, hidden_in, query_weight, key_weight, value_weight, query_bias, value_bias, mixer_weight, mixer_bias,
    first_gain, first_bias, inner_weight, inner_bias, outer_weight, outer_bias, second_gain, second_bias, lengths,
    cotangent,
):
    n, d = hidden_in.shape
    half = query_weight.shape[1]
    ff = inner_weight.shape[1]
    vec = jnp.concatenate(
        [
            query_bias, value_bias, mixer_bias, first_gain, first_bias, inner_bias, outer_bias, second_gain, second_bias,
            jnp.zeros(((V_ROWS - 9) * d,), BF),
        ]
    ).astype(F32).reshape(V_ROWS, d)
    heads = [query_weight, key_weight, value_weight, jnp.concatenate([mixer_weight[:, :half], mixer_weight[:, half:]])]
    sixteenth = d // 16
    h_out = jnp.concatenate(
        [piece(heads, (CORE, FAR, NEAR), 0, sixteenth), piece(heads, (CORE, NEAR, FAR), d // 2, sixteenth)]
    )
    i_out = jnp.concatenate(
        [
            piece([inner_weight], (CORE, FAR, NEAR), 0, sixteenth),
            piece([inner_weight], (CORE, NEAR, FAR), d // 2, sixteenth),
        ]
    )
    eighth = ff // 8
    o_out = jnp.concatenate(
        [piece([outer_weight], (CORE, NEAR), 0, eighth), piece([outer_weight], (CORE, FAR), ff // 2, eighth)]
    )
    pvec = lax.ppermute(vec, "tensor", TENSOR_SWAP)
    h_out, pvec = tie(h_out, pvec)
    h0 = lax.ppermute(h_out, "tensor", TENSOR_SWAP)
    own = list(attn_fwd(lengths, hidden_in, query_weight, key_weight, value_weight, vec, 0, 2))
    h0, i_out, own[0] = tie(h0, i_out, own[0])
    i0 = lax.ppermute(i_out, "tensor", TENSOR_SWAP)
    ha, hb = h0[:sixteenth], h0[sixteenth:]
    hra, hrb = swap(ha, NEAR, n_dp), swap(hb, FAR, n_dp)
    qo, ko, vo, co, lgo = attn_fwd(
        lengths, hidden_in, query_weight, key_weight, value_weight, vec, 2, 2, own, (ha, hb)
    )
    hra, hrb, i0, co, o_out = tie(hra, hrb, i0, co, o_out)
    ha, hb = in_order(NEAR, ha, hra), in_order(FAR, hb, hrb)
    hra, hrb = swap(ha, FAR, n_dp), swap(hb, NEAR, n_dp)
    o0 = lax.ppermute(o_out, "tensor", TENSOR_SWAP)
    ia, ib = i0[:sixteenth], i0[sixteenth:]
    ira, irb = swap(ia, NEAR, n_dp), swap(ib, FAR, n_dp)
    ha, hb = in_order(FAR, ha, hra), in_order(NEAR, hb, hrb)
    hra, hrb = swap(ha, CORE, n_dp), swap(hb, CORE, n_dp)
    ha, hb, ira, irb = tie(ha, hb, ira, irb)
    ia, ib = in_order(NEAR, ia, ira), in_order(FAR, ib, irb)
    ira, irb = swap(ia, FAR, n_dp), swap(ib, NEAR, n_dp)
    wqp, wkp, wvp, wmp = assemble(True, ha, hra, hb, hrb)
    peer = list(attn_fwd(lengths, hidden_in, wqp, wkp, wvp, pvec, 0, 2, None, (ia, ib)))
    ira, irb, o0, peer[0] = tie(ira, irb, o0, peer[0])
    ia, ib = in_order(FAR, ia, ira), in_order(NEAR, ib, irb)
    ira, irb = swap(ia, CORE, n_dp), swap(ib, CORE, n_dp)
    oa, ob = o0[:eighth], o0[eighth:]
    ora, orb = swap(oa, NEAR, n_dp), swap(ob, FAR, n_dp)
    qp, kp, vp, cp, lgp = attn_fwd(lengths, hidden_in, wqp, wkp, wvp, pvec, 2, 2, peer, (ia, ib, oa, ob))
    ora, orb, cp = tie(ora, orb, cp)
    oa, ob = in_order(NEAR, oa, ora), in_order(FAR, ob, orb)
    ora, orb = swap(oa, CORE, n_dp), swap(ob, CORE, n_dp)
    (wip,) = assemble(False, ia, ira, ib, irb)
    (wop,) = assemble(False, oa, ora, ob, orb)
    layer_out, x, low, gs, lo, gpo, gpp, owg, osums = ff_fwd(
        lengths, hidden_in, co, cp, cotangent, mixer_weight, wmp, inner_weight, wip, outer_weight, wop, vec, pvec
    )
    o = swap(away(owg, CORE), CORE, n_dp)
    opart, iwg, ibg = ff_bwd_own(lo, low, gpo, inner_weight, outer_weight)
    o, owg, iwg = tie(o, owg, iwg)
    i = swap(away(iwg, CORE), CORE, n_dp)
    o1 = kept(owg, CORE) + o
    o_out = away(o1, NEAR)
    o = swap(o_out, NEAR, n_dp)
    gm, lm, mwg, isums = ff_bwd_peer(lo, gs, x, gpp, opart, co, wip, wop, vec, o_out)
    o, i, lm = tie(o, i, lm)
    o2 = kept(o1, NEAR) + o
    o_out = away(o2, FAR)
    o = swap(o_out, FAR, n_dp)
    i1 = kept(iwg, CORE) + i
    i_out = away(i1, NEAR)
    i = swap(i_out, NEAR, n_dp)
    own = (lengths, lm, mixer_weight, qo, ko, vo, lgo, query_weight, key_weight, value_weight)
    part, hg = attn_bwd(True, 0, 2, *own, (hidden_in, mwg, isums, ibg, osums), None, (o_out, i_out))
    o, hg = tie(o, hg)
    o3 = kept(o2, FAR) + o
    o = swap(o3, 2 * FAR, n_dp) if n_dp > 2 * FAR else jnp.zeros_like(o3)
    part, hg = attn_bwd(True, 2, 2, *own, (hidden_in, hg), part, (o3,))
    i, o, hg = tie(i, o, hg)
    h = swap(away(hg, CORE), CORE, n_dp)
    i2 = kept(i1, NEAR) + i
    i_out = away(i2, FAR)
    i = swap(i_out, FAR, n_dp)
    o = beyond(o3 + o, n_dp)
    o_ = swap(o, FAR, n_dp)
    h1 = kept(hg, CORE) + h
    ha, hb = h1[:, :d], h1[:, d:]
    ha_out, hb_out = away(ha, NEAR), away(hb, FAR)
    hra, hrb = swap(ha_out, NEAR, n_dp), swap(hb_out, FAR, n_dp)
    peer = (lengths, lm, wmp, qp, kp, vp, lgp, wqp, wkp, wvp)
    (input_grad,) = attn_bwd(False, 0, 2, *peer, (gm, part), None, (o, i_out, ha_out, hb_out))
    hra, hrb, i, o_, input_grad = tie(hra, hrb, i, o_, input_grad)
    ha, hb = kept(ha, NEAR) + hra, kept(hb, FAR) + hrb
    ha_out, hb_out = away(ha, FAR), away(hb, NEAR)
    hra, hrb = swap(ha_out, FAR, n_dp), swap(hb_out, NEAR, n_dp)
    i3 = kept(i2, FAR) + i
    i = swap(i3, 2 * FAR, n_dp) if n_dp > 2 * FAR else jnp.zeros_like(i3)
    o = in_order(FAR, o, o_)
    o_ = swap(o, NEAR, n_dp)
    (input_grad,) = attn_bwd(False, 2, 2, *peer, (gm, part), input_grad, (ha_out, hb_out, i3, o))
    hra, hrb, i, o_, input_grad = tie(hra, hrb, i, o_, input_grad)
    h = jnp.concatenate([kept(ha, FAR) + hra, kept(hb, NEAR) + hrb])
    if n_dp > 2 * FAR:
        h = h + swap(h, 2 * FAR, n_dp)
    h = beyond(h, n_dp)
    i = beyond(i3 + i, n_dp)
    i = in_order(FAR, i, swap(i, FAR, n_dp))
    o = in_order(NEAR, o, o_)
    owg = in_order(CORE, o, swap(o, CORE, n_dp))
    i = in_order(NEAR, i, swap(i, NEAR, n_dp))
    iwg = in_order(CORE, i, swap(i, CORE, n_dp))
    rows = h.shape[0] // 2
    ha, hb = h[:rows], h[rows:]
    ha, hb = in_order(FAR, ha, swap(ha, FAR, n_dp)), in_order(NEAR, hb, swap(hb, NEAR, n_dp))
    ha, hb = in_order(NEAR, ha, swap(ha, NEAR, n_dp)), in_order(FAR, hb, swap(hb, FAR, n_dp))
    hg = jnp.concatenate(
        [in_order(CORE, ha, swap(ha, CORE, n_dp)), in_order(CORE, hb, swap(hb, CORE, n_dp))], axis=1
    )
    small = hg[d : d + 5].reshape(10, d)
    return (
        layer_out, input_grad, hg[:d, :half], hg[:d, half : 2 * half], hg[:d, 2 * half : 3 * half], small[0, :half],
        small[0, half:], jnp.concatenate([hg[:half, 3 * half :], hg[half:d, 3 * half :]], axis=1), small[1], small[2],
        small[3], iwg, small[4:6].reshape(ff), owg, small[6], small[7], small[8],
    )


def solution(mesh):
    col, row, rep = P(None, "tensor"), P("tensor", None), P()
    vec, tok = P("tensor"), P("dp", None)
    return jax.shard_map(
        partial(local, mesh.shape["dp"]),
        mesh=mesh,
        in_specs=(tok, col, col, col, vec, vec, row, rep, rep, rep, col, vec, row, rep, rep, rep, tok, tok),
        out_specs=(tok, tok, col, col, col, vec, vec, row, rep, rep, rep, col, vec, row, rep, rep, rep),
        check_vma=False,
    )
```

```python
import math
from functools import partial

import jax
import jax.numpy as jnp
from jax import lax
from jax.experimental import pallas as pl
from jax.experimental.pallas import tpu as pltpu
from jax.sharding import PartitionSpec as P

HD = 64
MAXLEN = 512
EPSILON = 1e-06
INV_SQRT2 = 1.0 / math.sqrt(2.0)
INV_SQRT_2PI = 1.0 / math.sqrt(2.0 * math.pi)
NEG = -1e30
FWD_GROUP = (1, 6, 6)
BWD_GROUP = (2, 6, 6)
BF = jnp.bfloat16
F32 = jnp.float32
VMEM_LIMIT = 56 * 1024 * 1024
PAD = 32
V_QV, V_MB, V_FG, V_FB, V_IB, V_OB, V_SG, V_SB = (0, 0), (0, 1), (1, 0), (1, 1), 2, (3, 0), (3, 1), (4, 0)


def vector(ref, place):
    row, side = place
    d = ref.shape[1] // 2
    return ref[row : row + 1, side * d : (side + 1) * d]


def dot(a, b):
    return lax.dot_general(a, b, (((1,), (0,)), ((), ())), preferred_element_type=F32)


def dot_bt(a, b):
    return lax.dot_general(a, b, (((1,), (1,)), ((), ())), preferred_element_type=F32)


def dot_at(a, b):
    return lax.dot_general(a, b, (((0,), (0,)), ((), ())), preferred_element_type=F32)


def core_halves(size):
    core = lax.axis_index("dp") & 1
    return [pl.ds(pl.multiple_of(side * size, 128), size) for side in (core, 1 - core)]


def head_lanes(rows):
    return lax.broadcasted_iota(jnp.int32, (rows, 2 * HD), 1) < HD


def params(**kw):
    return pltpu.CompilerParams(vmem_limit_bytes=VMEM_LIMIT, **kw)


def full(shape):
    return pl.BlockSpec(shape, lambda b: (0,) * len(shape), pipeline_mode=pl.Buffered(1))


def rows_spec(cols, start=0):
    return pl.BlockSpec((MAXLEN, cols), lambda b: (b + start, 0))


SMEM = pl.BlockSpec(memory_space=pltpu.SMEM)
ANY = pl.BlockSpec(memory_space=pl.ANY)


def cost(us):
    return pl.CostEstimate(flops=int(us * 1e9), bytes_accessed=1_000_000, transcendentals=0)


def attn_fwd_kernel(start, skip, len_ref, h_ref, wq_ref, wk_ref, wv_ref, vec_ref, *rest):
    q_ref, k_ref, v_ref, c_ref, l_ref = rest[skip:]
    half = wq_ref.shape[1]
    pairs = half // (2 * HD)
    b = pl.program_id(0) + start
    h = h_ref[...]
    q_ref[...] = (dot(h, wq_ref[...]) + vec_ref[0:1, :half]).astype(BF)
    k_ref[...] = dot(h, wk_ref[...]).astype(BF)
    v_ref[...] = (dot(h, wv_ref[...]) + vec_ref[0:1, half : 2 * half]).astype(BF)
    l_ref[...] = jnp.zeros_like(l_ref)
    for kind in range(3):

        @pl.when(lax.rem(b, 3) == kind)
        def _():
            span = MAXLEN >> kind
            low_lanes = head_lanes(span)
            lane = lax.broadcasted_iota(jnp.int32, (span, 128), 1)
            for seq in range(1 << kind):
                rows = slice(seq * span, (seq + 1) * span)
                live = lax.broadcasted_iota(jnp.int32, (1, span), 1) < len_ref[b, seq]
                bias = jnp.where(live, 0.0, NEG)
                logs = jnp.zeros((span, 128), F32)
                outs = []
                group = FWD_GROUP[kind]
                for first in range(0, 2 * pairs, group):
                    heads = range(first, first + group)
                    cols = [slice(head // 2 * 2 * HD, (head // 2 + 1) * 2 * HD) for head in heads]
                    qs = [
                        jnp.where(low_lanes if head % 2 == 0 else ~low_lanes, q_ref[rows, at] * BF(0.125), BF(0))
                        for head, at in zip(heads, cols)
                    ]
                    scores = [dot_bt(q, k_ref[rows, at]) + bias for q, at in zip(qs, cols)]
                    peaks = [jnp.max(x, axis=-1, keepdims=True) for x in scores]
                    exps = [jnp.exp(x - m) for x, m in zip(scores, peaks)]
                    totals = [jnp.sum(x, axis=-1, keepdims=True) for x in exps]
                    probs = [(x * (1.0 / z)).astype(BF) for x, z in zip(exps, totals)]
                    outs += [dot(p, v_ref[rows, at]) for p, at in zip(probs, cols)]
                    for head, m, z in zip(heads, peaks, totals):
                        logs = jnp.where(lane == head, m + jnp.log(z), logs)
                for pair in range(pairs):
                    both = jnp.where(low_lanes, outs[2 * pair], outs[2 * pair + 1])
                    c_ref[rows, pair * 2 * HD : (pair + 1) * 2 * HD] = both.astype(BF)
                l_ref[:, rows] = logs.T[:8]


def attn_fwd(lengths, hidden, wq, wk, wv, vec, start, count, prior=None, after=()):
    n, d = hidden.shape
    half = wq.shape[1]
    blocks = n // MAXLEN
    wide = jax.ShapeDtypeStruct((n, half), BF)
    prior = list(prior or ())
    extra = prior + list(after)
    return pl.pallas_call(
        partial(attn_fwd_kernel, start, len(extra)),
        grid=(count,),
        in_specs=[
            SMEM, rows_spec(d, start), full((d, half)), full((d, half)), full((d, half)), full(vec.shape),
            *[ANY] * len(extra),
        ],
        out_specs=[rows_spec(half, start)] * 4 + [pl.BlockSpec((8, MAXLEN), lambda b: (b + start, 0))],
        out_shape=[wide] * 4 + [jax.ShapeDtypeStruct((8 * blocks, MAXLEN), F32)],
        input_output_aliases={6 + i: i for i in range(len(prior))},
        compiler_params=params(),
        cost_estimate=cost(7 * count),
        name="attn_fwd",
    )(lengths, hidden, wq, wk, wv, vec, *extra)


def live_column(len_ref, b):
    pos = lax.broadcasted_iota(jnp.int32, (MAXLEN, 1), 0)
    kind = lax.rem(b, 3)
    shift = 9 - kind
    seg = lax.shift_right_logical(pos, shift)
    off = pos - lax.shift_left(seg, shift)
    picked = jnp.full((MAXLEN, 1), len_ref[b, 0], jnp.int32)
    for slot in range(1, 4):
        picked = jnp.where(seg == slot, len_ref[b, slot], picked)
    return (off < picked).astype(F32)


def norm_stats(x):
    center = x - jnp.mean(x, axis=-1, keepdims=True)
    inverse = lax.rsqrt(jnp.mean(center * center, axis=-1, keepdims=True) + EPSILON)
    return center * inverse, inverse


def accumulate(ref, value, first_step):
    @pl.when(first_step)
    def _():
        ref[...] = value

    @pl.when(jnp.logical_not(first_step))
    def _():
        ref[...] += value


def ff_fwd_kernel(
    len_ref, h_ref, co_ref, cp_ref, cot_ref, wmo_ref, wmp_ref, wio_ref, wip_ref, woo_ref, wop_ref, vec_ref, pvec_ref,
    out_ref, x_ref, low_ref, gs_ref, lo_ref, gpo_ref, gpp_ref, owk_ref, owa_ref, sums_ref, act_ref, pa_ref, pb_ref,
):
    b = pl.program_id(0)
    d = h_ref.shape[1]
    ff = wio_ref.shape[1]
    width = 512
    pa_ref[...] = dot(co_ref[...], wmo_ref[...])
    pb_ref[...] = dot(cp_ref[...], wmp_ref[...])
    mixed = (pa_ref[...] + pb_ref[...]) + vector(vec_ref, V_MB)
    x = h_ref[...].astype(F32) + mixed
    x_ref[...] = x
    n1, _ = norm_stats(x)
    first = n1 * vector(vec_ref, V_FG) + vector(vec_ref, V_FB)
    low = first.astype(BF)
    low_ref[...] = low
    for wi, wo, vec, gp_ref, part_ref, keep in (
        (wio_ref, woo_ref, vec_ref, gpo_ref, pa_ref, True),
        (wip_ref, wop_ref, pvec_ref, gpp_ref, pb_ref, False),
    ):
        part = None
        for c in range(ff // width):
            cols = slice(c * width, (c + 1) * width)
            inner = dot(low, wi[:, cols]) + vec[V_IB : V_IB + 1, cols]
            cdf = 0.5 * (1.0 + lax.erf(inner * INV_SQRT2))
            gp_ref[:, cols] = cdf + inner * (jnp.exp(-0.5 * inner * inner) * INV_SQRT_2PI)
            active = (inner * cdf).astype(BF)
            if keep:
                act_ref[:, cols] = active
            term = dot(active, wo[cols, :])
            part = term if part is None else part + term
        part_ref[...] = part
    r = first + ((pa_ref[...] + pb_ref[...]) + vector(vec_ref, V_OB))
    n2, inv2 = norm_stats(r)
    gain = vector(vec_ref, V_SG)
    out_ref[...] = (n2 * gain + vector(vec_ref, V_SB)).astype(BF)
    g = cot_ref[...].astype(F32) * live_column(len_ref, b)
    scaled = g * gain
    gs = inv2 * (
        scaled - jnp.mean(scaled, axis=-1, keepdims=True) - n2 * jnp.mean(scaled * n2, axis=-1, keepdims=True)
    )
    gs_ref[...] = gs
    lo = gs.astype(BF)
    lo_ref[...] = lo
    sums = jnp.concatenate(
        [
            jnp.sum(gs, axis=0, keepdims=True),
            jnp.sum(g * n2, axis=0, keepdims=True),
            jnp.sum(g, axis=0, keepdims=True),
            jnp.zeros((5, d), F32),
        ],
        axis=0,
    )
    accumulate(sums_ref, sums, b == 0)
    for ref, cols in zip((owk_ref, owa_ref), core_halves(ff // 2)):
        accumulate(ref, dot_at(act_ref[:, cols], lo), b == 0)


def ff_fwd(lengths, hidden, co, cp, cot, wmo, wmp, wio, wip, woo, wop, vec, pvec):
    n, d = hidden.shape
    half = co.shape[1]
    ff = wio.shape[1]
    return pl.pallas_call(
        ff_fwd_kernel,
        grid=(n // MAXLEN,),
        in_specs=[
            SMEM, rows_spec(d), rows_spec(half), rows_spec(half), rows_spec(d), full((half, d)), full((half, d)),
            full((d, ff)), full((d, ff)), full((ff, d)), full((ff, d)), full(vec.shape), full(pvec.shape),
        ],
        out_specs=[
            rows_spec(d), rows_spec(d), rows_spec(d), rows_spec(d), rows_spec(d), rows_spec(ff), rows_spec(ff),
            full((ff // 2, d)), full((ff // 2, d)), full((8, d)),
        ],
        out_shape=[
            jax.ShapeDtypeStruct((n, d), BF),
            jax.ShapeDtypeStruct((n, d), F32),
            jax.ShapeDtypeStruct((n, d), BF),
            jax.ShapeDtypeStruct((n, d), F32),
            jax.ShapeDtypeStruct((n, d), BF),
            jax.ShapeDtypeStruct((n, ff), F32),
            jax.ShapeDtypeStruct((n, ff), F32),
            jax.ShapeDtypeStruct((ff // 2, d), F32),
            jax.ShapeDtypeStruct((ff // 2, d), F32),
            jax.ShapeDtypeStruct((8, d), F32),
        ],
        scratch_shapes=[pltpu.VMEM((MAXLEN, ff), BF), pltpu.VMEM((MAXLEN, d), F32), pltpu.VMEM((MAXLEN, d), F32)],
        compiler_params=params(),
        cost_estimate=cost(58),
        name="ff_fwd",
    )(lengths, hidden, co, cp, cot, wmo, wmp, wio, wip, woo, wop, vec, pvec)


def ff_bwd_half(lo, wi_ref, wo_ref, gp_ref, gi_ref, part_ref):
    width = 512
    part = None
    for c in range(wi_ref.shape[1] // width):
        cols = slice(c * width, (c + 1) * width)
        gi = (dot_bt(lo, wo_ref[cols, :]) * gp_ref[:, cols]).astype(BF)
        if gi_ref is not None:
            gi_ref[:, cols] = gi
        term = dot_bt(gi, wi_ref[:, cols])
        part = term if part is None else part + term
    part_ref[...] = part


def ff_bwd_own_kernel(skip, lo_ref, low_ref, gp_ref, wi_ref, wo_ref, *rest):
    part_ref, iwk_ref, iwa_ref, isum_ref, gi_ref = rest[skip:]
    b = pl.program_id(0)
    ff_bwd_half(lo_ref[...], wi_ref, wo_ref, gp_ref, gi_ref, part_ref)
    gi = gi_ref[...]
    for ref, cols in zip((iwk_ref, iwa_ref), core_halves(low_ref.shape[1] // 2)):
        accumulate(ref, dot_at(low_ref[:, cols], gi), b == 0)
    accumulate(isum_ref, jnp.sum(gi.astype(F32), axis=0, keepdims=True), b == 0)


def ff_bwd_own(lo, low, gp, wi, wo, *after):
    n, d = lo.shape
    ff = wi.shape[1]
    return pl.pallas_call(
        partial(ff_bwd_own_kernel, len(after)),
        grid=(n // MAXLEN,),
        in_specs=[rows_spec(d), rows_spec(d), rows_spec(ff), full((d, ff)), full((ff, d)), *[ANY] * len(after)],
        out_specs=[rows_spec(d), full((d // 2, ff)), full((d // 2, ff)), full((1, ff))],
        out_shape=[
            jax.ShapeDtypeStruct((n, d), F32),
            jax.ShapeDtypeStruct((d // 2, ff), F32),
            jax.ShapeDtypeStruct((d // 2, ff), F32),
            jax.ShapeDtypeStruct((1, ff), F32),
        ],
        scratch_shapes=[pltpu.VMEM((MAXLEN, ff), BF)],
        compiler_params=params(),
        cost_estimate=cost(26),
        name="ff_bwd_own",
    )(lo, low, gp, wi, wo, *after)


def ff_bwd_peer_kernel(
    skip, lo_ref, gs_ref, x_ref, gp_ref, opart_ref, co_ref, wi_ref, wo_ref, vec_ref, *rest
):
    gm_ref, lm_ref, mwg_ref, sums_ref, part_ref = rest[skip:]
    b = pl.program_id(0)
    d = lo_ref.shape[1]
    ff_bwd_half(lo_ref[...], wi_ref, wo_ref, gp_ref, None, part_ref)
    g = gs_ref[...] + (opart_ref[...] + part_ref[...])
    n1, inv1 = norm_stats(x_ref[...])
    scaled = g * vector(vec_ref, V_FG)
    gm = inv1 * (
        scaled - jnp.mean(scaled, axis=-1, keepdims=True) - n1 * jnp.mean(scaled * n1, axis=-1, keepdims=True)
    )
    gm_ref[...] = gm
    lm = gm.astype(BF)
    lm_ref[...] = lm
    sums = jnp.concatenate(
        [
            jnp.sum(gm, axis=0, keepdims=True),
            jnp.sum(g * n1, axis=0, keepdims=True),
            jnp.sum(g, axis=0, keepdims=True),
            jnp.zeros((5, d), F32),
        ],
        axis=0,
    )
    accumulate(sums_ref, sums, b == 0)
    accumulate(mwg_ref, dot_at(co_ref[...], lm), b == 0)


def ff_bwd_peer(lo, gs, x, gp, opart, co, wi, wo, vec, *after):
    n, d = lo.shape
    half = co.shape[1]
    ff = wi.shape[1]
    return pl.pallas_call(
        partial(ff_bwd_peer_kernel, len(after)),
        grid=(n // MAXLEN,),
        in_specs=[
            rows_spec(d), rows_spec(d), rows_spec(d), rows_spec(ff), rows_spec(d), rows_spec(half), full((d, ff)),
            full((ff, d)), full(vec.shape), *[ANY] * len(after),
        ],
        out_specs=[rows_spec(d), rows_spec(d), full((half, d)), full((8, d))],
        out_shape=[
            jax.ShapeDtypeStruct((n, d), F32),
            jax.ShapeDtypeStruct((n, d), BF),
            jax.ShapeDtypeStruct((half, d), F32),
            jax.ShapeDtypeStruct((8, d), F32),
        ],
        scratch_shapes=[pltpu.VMEM((MAXLEN, d), F32)],
        compiler_params=params(),
        cost_estimate=cost(25),
        name="ff_bwd_peer",
    )(lo, gs, x, gp, opart, co, wi, wo, vec, *after)


def attn_bwd_kernel(own, start, skip, len_ref, lm_ref, wm_ref, q_ref, k_ref, v_ref, l_ref, wq_ref, wk_ref, wv_ref, *rest):
    if own:
        given = 3 if start else 5
        h_ref, *given = rest[:given]
        part_ref, wk_out, wa_out, gc_ref, dq_ref, dk_ref, dv_ref = rest[len(given) + 1 + skip :]
    else:
        gm_ref, opart_ref = rest[:2]
        ig_ref, gc_ref, dq_ref, dk_ref, dv_ref, part_ref = rest[2 + skip :]
    half = wq_ref.shape[1]
    pairs = half // (2 * HD)
    b = pl.program_id(0) + start
    gc_ref[...] = dot_bt(lm_ref[...], wm_ref[...]).astype(BF)
    for kind in range(3):

        @pl.when(lax.rem(b, 3) == kind)
        def _():
            span = MAXLEN >> kind
            low_lanes = head_lanes(span)
            for seq in range(1 << kind):
                rows = slice(seq * span, (seq + 1) * span)
                live = lax.broadcasted_iota(jnp.int32, (span, 1), 0) < len_ref[b, seq]
                bias = jnp.where(live, 0.0, NEG)
                dqs, dks, dvs = [], [], []
                group = BWD_GROUP[kind]
                for first in range(0, 2 * pairs, group):
                    heads = range(first, first + group)
                    cols = [slice(head // 2 * 2 * HD, (head // 2 + 1) * 2 * HD) for head in heads]
                    masks = [low_lanes if head % 2 == 0 else ~low_lanes for head in heads]
                    qs = [q_ref[rows, at] * BF(0.125) for at in cols]
                    ups = [gc_ref[rows, at] for at in cols]
                    scores = [
                        dot_bt(k_ref[rows, at], jnp.where(mask, q, BF(0))) + bias for q, at, mask in zip(qs, cols, masks)
                    ]
                    dprobs = [
                        dot_bt(v_ref[rows, at], jnp.where(mask, up, BF(0))) for up, at, mask in zip(ups, cols, masks)
                    ]
                    probs = [jnp.exp(x - l_ref[head : head + 1, rows]) for x, head in zip(scores, heads)]
                    deltas = [jnp.sum(p * dp, axis=0, keepdims=True) for p, dp in zip(probs, dprobs)]
                    dscores = [(p * (dp - delta)).astype(BF) for p, dp, delta in zip(probs, dprobs, deltas)]
                    dvs += [dot(p.astype(BF), up) for p, up in zip(probs, ups)]
                    dks += [dot(ds, q) for ds, q in zip(dscores, qs)]
                    dqs += [dot_at(ds, k_ref[rows, at]) for ds, at in zip(dscores, cols)]
                for pair in range(pairs):
                    at = slice(pair * 2 * HD, (pair + 1) * 2 * HD)
                    dv_ref[rows, at] = jnp.where(low_lanes, dvs[2 * pair], dvs[2 * pair + 1]).astype(BF)
                    dk_ref[rows, at] = jnp.where(low_lanes, dks[2 * pair], dks[2 * pair + 1]).astype(BF)
                    dq = jnp.where(low_lanes, dqs[2 * pair], dqs[2 * pair + 1]) * 0.125
                    dq_ref[rows, at] = dq.astype(BF)

    dq, dk, dv = dq_ref[...], dk_ref[...], dv_ref[...]
    part = (dot_bt(dq, wq_ref[...]) + dot_bt(dk, wk_ref[...])) + dot_bt(dv, wv_ref[...])
    part_ref[...] = part
    if own:
        d = h_ref.shape[1]
        sums = jnp.concatenate(
            [jnp.sum(dq.astype(F32), axis=0, keepdims=True), jnp.sum(dv.astype(F32), axis=0, keepdims=True)], axis=1
        )
        first_step = b == start
        core = lax.axis_index("dp") & 1
        for side, (out, cols) in enumerate(zip((wk_out, wa_out), core_halves(half))):
            holds = (core == side).astype(F32)

            @pl.when(first_step)
            def _(side=side, out=out, cols=cols, holds=holds):
                if start:
                    out[...] = given[side][...]
                    return
                mwg_ref, fsum_ref, isum_ref, osum_ref = given
                pad = jnp.zeros((1, d), F32)
                top = jnp.concatenate([pad, fsum_ref[0:1, :]], axis=1)
                mid = jnp.concatenate([fsum_ref[1:2, :], fsum_ref[2:3, :]], axis=1)
                low = jnp.concatenate([osum_ref[0:1, :], osum_ref[1:2, :]], axis=1)
                end = jnp.concatenate([osum_ref[2:3, :], pad], axis=1)
                vectors = jnp.concatenate([top, mid, isum_ref[...], low, end, jnp.zeros((3, 2 * d), F32)], axis=0)
                out[:half, : 3 * half] = jnp.zeros((half, 3 * half), F32)
                out[:half, 3 * half :] = mwg_ref[:, cols]
                out[half : half + 8, :] = vectors * holds
                out[half + 8 :, :] = jnp.zeros((PAD - 8, 2 * d), F32)

            h = h_ref[:, cols]
            for i, grad in enumerate((dq, dk, dv)):
                out[:half, i * half : (i + 1) * half] += dot_at(h, grad)
            out[half : half + 1, :d] += sums * holds
    else:
        ig_ref[...] = (gm_ref[...] + (opart_ref[...] + part_ref[...])).astype(BF)


def attn_bwd(own, start, count, lengths, lm, wm, q, k, v, logs, wq, wk, wv, extra, prior=None, after=()):
    n, d = lm.shape
    half = wq.shape[1]
    after = ([] if prior is None else [prior]) + list(after)
    if own:
        extra_specs = [rows_spec(d, start)] + [full(x.shape) for x in extra[1:]]
        out_specs = [rows_spec(d, start)] + [full((half + PAD, 4 * half))] * 2
        out_shape = [jax.ShapeDtypeStruct((n, d), F32)] + [jax.ShapeDtypeStruct((half + PAD, 4 * half), F32)] * 2
    else:
        extra_specs = [rows_spec(d, start)] * 2
        out_specs = [rows_spec(d, start)]
        out_shape = [jax.ShapeDtypeStruct((n, d), BF)]
    return pl.pallas_call(
        partial(attn_bwd_kernel, own, start, len(after)),
        grid=(count,),
        in_specs=[
            SMEM, rows_spec(d, start), full((half, d)), rows_spec(half, start), rows_spec(half, start),
            rows_spec(half, start), pl.BlockSpec((8, MAXLEN), lambda b: (b + start, 0)), full((d, half)),
            full((d, half)), full((d, half)), *extra_specs, *[ANY] * len(after),
        ],
        out_specs=out_specs,
        out_shape=out_shape,
        input_output_aliases={} if prior is None else {10 + len(extra): 0},
        scratch_shapes=[pltpu.VMEM((MAXLEN, half), BF)] * 4 + ([] if own else [pltpu.VMEM((MAXLEN, d), F32)]),
        compiler_params=params(),
        cost_estimate=cost(12 * count if own else 40),
        name="attn_bwd_own" if own else "attn_bwd_peer",
    )(lengths, lm, wm, q, k, v, logs, wq, wk, wv, *extra, *after)


CORE, NEAR, FAR = 1, 2, 4
TENSOR_SWAP = [(0, 1), (1, 0)]


def bit_of(mask):
    return (lax.axis_index("dp") & mask) != 0


def swap(x, mask, n_dp):
    return lax.ppermute(x, "dp", [(i, i ^ mask) for i in range(n_dp)])


def in_order(mask, mine, other):
    return jnp.where(bit_of(mask), jnp.concatenate([other, mine]), jnp.concatenate([mine, other]))


def away(x, mask):
    rows = x.shape[0] // 2
    return lax.dynamic_slice_in_dim(x, jnp.where(bit_of(mask), 0, rows), rows, 0)


def kept(x, mask):
    rows = x.shape[0] // 2
    return lax.dynamic_slice_in_dim(x, jnp.where(bit_of(mask), rows, 0), rows, 0)


def exchange(x, mask, n_dp):
    return swap(x, mask, n_dp) if mask < n_dp else jnp.zeros_like(x)


def join_kernel(mine_ref, other_ref, out_ref):
    rows = mine_ref.shape[0]
    core = lax.axis_index("dp") & 1
    out_ref[pl.ds(pl.multiple_of(core * rows, 8), rows), :] = mine_ref[...]
    out_ref[pl.ds(pl.multiple_of((1 - core) * rows, 8), rows), :] = other_ref[...]


def join(mine, other):
    return pl.pallas_call(
        join_kernel,
        out_shape=jax.ShapeDtypeStruct((2 * mine.shape[0], mine.shape[1]), mine.dtype),
        compiler_params=params(),
        cost_estimate=cost(0.1),
        name="join",
    )(mine, other)


def beyond(x, n_dp):
    mask = 4 * FAR
    while mask < n_dp:
        x = x + swap(x, mask, n_dp)
        mask *= 2
    return x


def piece(arrays, masks, base, rows):
    index = jnp.int32(0)
    for mask in masks:
        index = index * 2 + bit_of(mask).astype(jnp.int32)
    cut = [lax.dynamic_slice_in_dim(a, base + index * rows, rows, 0) for a in arrays]
    return jnp.concatenate(cut, axis=1).astype(F32)


def tie(*arrays):
    return lax.optimization_barrier(arrays)


def prepare_kernel(*refs):
    weights, vectors, (vec_ref, out_ref) = refs[:4], refs[4:-2], refs[-2:]
    d = vec_ref.shape[1] // 2
    qb, vb, mb, fg, fb, ib, ob, sg, sb = [ref[...].astype(F32).reshape(1, -1) for ref in vectors]
    zero = jnp.zeros((1, d), F32)
    rows = [(qb, vb, mb), (fg, fb), (ib,), (ob, sg), (sb, zero)]
    vec = jnp.concatenate(
        [jnp.concatenate(row, axis=1) for row in rows] + [jnp.zeros((3, 2 * d), F32)], axis=0
    )
    vec_ref[...] = vec
    me = lax.axis_index("dp")
    core, near, far = me & 1, (me >> 1) & 1, (me >> 2) & 1
    half = d // 2
    rows = d // 16
    for base, index in ((0, core * 4 + far * 2 + near), (8 * rows, core * 4 + near * 2 + far)):
        at = pl.ds(pl.multiple_of(base + index * rows, 16), rows)
        to = slice(base // 8, base // 8 + rows)
        for i in range(3):
            out_ref[to, i * half : (i + 1) * half] = weights[i][at, :].astype(F32)
        at = pl.ds(pl.multiple_of(index * rows, 16), rows)
        cols = slice(0, half) if base == 0 else slice(half, d)
        out_ref[to, 3 * half :] = weights[3][at, cols].astype(F32)
    out_ref[2 * rows :, :] = vec


def prepare(weights, vectors):
    d = weights[0].shape[0]
    return pl.pallas_call(
        prepare_kernel,
        out_shape=[jax.ShapeDtypeStruct((8, 2 * d), F32), jax.ShapeDtypeStruct((d // 8 + 8, 2 * d), F32)],
        compiler_params=params(),
        cost_estimate=cost(2),
        name="prepare",
    )(*weights, *vectors)


def finish_kernel(a_ref, ra_ref, b_ref, rb_ref, q_ref, k_ref, v_ref, m_ref, *vectors):
    half = m_ref.shape[0]
    d = 2 * half
    mine, other = core_halves(half)
    core = lax.axis_index("dp") & 1
    for cols, x_ref, y_ref in ((mine, a_ref, b_ref), (other, ra_ref, rb_ref)):
        q_ref[cols, :] = x_ref[:half, :half]
        k_ref[cols, :] = x_ref[:half, half:]
        v_ref[cols, :] = y_ref[:half, :half]
        m_ref[:, cols] = y_ref[:half, half:]
    pad = slice(half, half + 8)
    left = jnp.where(core == 0, a_ref[pad, :], ra_ref[pad, :])
    right = jnp.where(core == 0, b_ref[pad, :], rb_ref[pad, :])
    rows = (
        left[0:1, :half], left[0:1, half:], right[0:1], left[1:2], right[1:2],
        jnp.concatenate([left[2:3], right[2:3]], axis=1), left[3:4], right[3:4], left[4:5],
    )
    for ref, row in zip(vectors, rows):
        ref[...] = row.reshape(-1)


def finish(a, ra, b, rb):
    d = a.shape[1]
    half = d // 2
    return pl.pallas_call(
        finish_kernel,
        out_shape=[jax.ShapeDtypeStruct((d, half), F32)] * 3
        + [jax.ShapeDtypeStruct((half, d), F32)]
        + [jax.ShapeDtypeStruct((size,), F32) for size in (half, half, d, d, d, 2 * d, d, d, d)],
        compiler_params=params(),
        cost_estimate=cost(0.1),
        name="finish",
    )(a, ra, b, rb)


def assemble_kernel(square, a_ref, ra_ref, b_ref, rb_ref, *outs):
    rows = a_ref.shape[0]
    odd = lax.axis_index("dp") & CORE
    for base, mine, other in ((0, a_ref, ra_ref), (2 * rows, b_ref, rb_ref)):
        for ref, side in ((mine, odd), (other, 1 - odd)):
            at = pl.ds(pl.multiple_of(base + side * rows, 16), rows)
            if not square:
                outs[0][at, :] = ref[...].astype(BF)
                continue
            half = ref.shape[1] // 4
            for i in range(3):
                outs[i][at, :] = ref[:, i * half : (i + 1) * half].astype(BF)
            at = pl.ds(pl.multiple_of(side * rows, 16), rows)
            left = base == 0
            cols = slice(0, half) if left else slice(half, 2 * half)
            outs[3][at, cols] = ref[:, 3 * half :].astype(BF)


def assemble(square, a, ra, b, rb):
    rows, cols = 4 * a.shape[0], a.shape[1]
    half = cols // 4
    if square:
        shapes = [(rows, half)] * 3 + [(rows // 2, 2 * half)]
    else:
        shapes = [(rows, cols)]
    return pl.pallas_call(
        partial(assemble_kernel, square),
        out_shape=[jax.ShapeDtypeStruct(shape, BF) for shape in shapes],
        compiler_params=params(),
        cost_estimate=cost(4),
        name="assemble",
    )(a, ra, b, rb)


def local(
    n_dp, hidden_in, query_weight, key_weight, value_weight, query_bias, value_bias, mixer_weight, mixer_bias,
    first_gain, first_bias, inner_weight, inner_bias, outer_weight, outer_bias, second_gain, second_bias, lengths,
    cotangent,
):
    n, d = hidden_in.shape
    half = query_weight.shape[1]
    ff = inner_weight.shape[1]
    vec, h_out = prepare(
        (query_weight, key_weight, value_weight, mixer_weight),
        (
            query_bias, value_bias, mixer_bias, first_gain, first_bias, inner_bias, outer_bias, second_gain,
            second_bias,
        ),
    )
    sixteenth = d // 16
    i_out = jnp.concatenate(
        [
            piece([inner_weight], (CORE, FAR, NEAR), 0, sixteenth),
            piece([inner_weight], (CORE, NEAR, FAR), d // 2, sixteenth),
        ]
    )
    eighth = ff // 8
    o_out = jnp.concatenate(
        [piece([outer_weight], (CORE, NEAR), 0, eighth), piece([outer_weight], (CORE, FAR), ff // 2, eighth)]
    )
    h0 = lax.ppermute(h_out, "tensor", TENSOR_SWAP)
    own = list(attn_fwd(lengths, hidden_in, query_weight, key_weight, value_weight, vec, 0, 2))
    h0, i_out, own[0] = tie(h0, i_out, own[0])
    i0 = lax.ppermute(i_out, "tensor", TENSOR_SWAP)
    ha, hb, pvec = h0[:sixteenth], h0[sixteenth : 2 * sixteenth], h0[2 * sixteenth :]
    hra, hrb = swap(ha, NEAR, n_dp), swap(hb, FAR, n_dp)
    qo, ko, vo, co, lgo = attn_fwd(
        lengths, hidden_in, query_weight, key_weight, value_weight, vec, 2, 2, own, (ha, hb)
    )
    hra, hrb, i0, co, o_out = tie(hra, hrb, i0, co, o_out)
    ha, hb = in_order(NEAR, ha, hra), in_order(FAR, hb, hrb)
    hra, hrb = swap(ha, FAR, n_dp), swap(hb, NEAR, n_dp)
    o0 = lax.ppermute(o_out, "tensor", TENSOR_SWAP)
    ia, ib = i0[:sixteenth], i0[sixteenth:]
    ira, irb = swap(ia, NEAR, n_dp), swap(ib, FAR, n_dp)
    ha, hb = in_order(FAR, ha, hra), in_order(NEAR, hb, hrb)
    hra, hrb = swap(ha, CORE, n_dp), swap(hb, CORE, n_dp)
    ha, hb, ira, irb = tie(ha, hb, ira, irb)
    ia, ib = in_order(NEAR, ia, ira), in_order(FAR, ib, irb)
    ira, irb = swap(ia, FAR, n_dp), swap(ib, NEAR, n_dp)
    wqp, wkp, wvp, wmp = assemble(True, ha, hra, hb, hrb)
    peer = list(attn_fwd(lengths, hidden_in, wqp, wkp, wvp, pvec, 0, 2, None, (ia, ib)))
    ira, irb, o0, peer[0] = tie(ira, irb, o0, peer[0])
    ia, ib = in_order(FAR, ia, ira), in_order(NEAR, ib, irb)
    ira, irb = swap(ia, CORE, n_dp), swap(ib, CORE, n_dp)
    oa, ob = o0[:eighth], o0[eighth:]
    ora, orb = swap(oa, NEAR, n_dp), swap(ob, FAR, n_dp)
    qp, kp, vp, cp, lgp = attn_fwd(lengths, hidden_in, wqp, wkp, wvp, pvec, 2, 2, peer, (ia, ib, oa, ob))
    ora, orb, cp = tie(ora, orb, cp)
    oa, ob = in_order(NEAR, oa, ora), in_order(FAR, ob, orb)
    ora, orb = swap(oa, CORE, n_dp), swap(ob, CORE, n_dp)
    (wip,) = assemble(False, ia, ira, ib, irb)
    (wop,) = assemble(False, oa, ora, ob, orb)
    layer_out, x, low, gs, lo, gpo, gpp, owk, owa, osums = ff_fwd(
        lengths, hidden_in, co, cp, cotangent, mixer_weight, wmp, inner_weight, wip, outer_weight, wop, vec, pvec
    )
    o, lo = tie(swap(owa, CORE, n_dp), lo)
    o1 = owk + o
    o_out = away(o1, NEAR)
    o = swap(o_out, NEAR, n_dp)
    opart, iwk, iwa, ibg = ff_bwd_own(lo, low, gpo, inner_weight, outer_weight, o_out)
    o, opart, iwa = tie(o, opart, iwa)
    i, opart = tie(swap(iwa, CORE, n_dp), opart)
    i1 = iwk + i
    i_out = away(i1, NEAR)
    i = swap(i_out, NEAR, n_dp)
    o2 = kept(o1, NEAR) + o
    o_out = away(o2, FAR)
    o = swap(o_out, FAR, n_dp)
    gm, lm, mwg, isums = ff_bwd_peer(lo, gs, x, gpp, opart, co, wip, wop, vec, o_out, i_out)
    o, i, lm = tie(o, i, lm)
    i2 = kept(i1, NEAR) + i
    i_out = away(i2, FAR)
    i = swap(i_out, FAR, n_dp)
    o3 = kept(o2, FAR) + o
    o3, i_out = tie(o3, i_out)
    o = exchange(o3, 2 * FAR, n_dp)
    own = (lengths, lm, mixer_weight, qo, ko, vo, lgo, query_weight, key_weight, value_weight)
    part, hk, ha = attn_bwd(True, 0, 2, *own, (hidden_in, mwg, isums, ibg, osums), None, (o3, i_out))
    o, i, part = tie(o, i, part)
    o = beyond(o3 + o, n_dp)
    o_ = swap(o, FAR, n_dp)
    i3 = kept(i2, FAR) + i
    i3, o = tie(i3, o)
    i = exchange(i3, 2 * FAR, n_dp)
    part, hk, ha = attn_bwd(True, 2, 2, *own, (hidden_in, hk, ha), part, (o, i3))
    h = swap(ha, CORE, n_dp)
    o_, ha = tie(o_, ha)
    o = in_order(FAR, o, o_)
    cut = o.shape[0] // 2
    oa_, ob = swap(o[:cut], NEAR, n_dp), o[cut:]
    peer = (lengths, lm, wmp, qp, kp, vp, lgp, wqp, wkp, wvp)
    (ig,) = attn_bwd(False, 0, 1, *peer, (gm, part), None, (o,))
    h, i, ig = tie(h, i, ig)
    h1 = hk + h
    ha, hb = h1[:, :d], h1[:, d:]
    ha_out, hb_out = away(ha, NEAR), away(hb, FAR)
    hra, hrb = swap(ha_out, NEAR, n_dp), swap(hb_out, FAR, n_dp)
    i = beyond(i3 + i, n_dp)
    i, hb_out = tie(i, hb_out)
    i_ = swap(i, FAR, n_dp)
    (ig,) = attn_bwd(False, 1, 1, *peer, (gm, part), ig, (ha_out, hb_out, i))
    hra, hrb, ob, ig = tie(hra, hrb, ob, ig)
    ha, hb = kept(ha, NEAR) + hra, kept(hb, FAR) + hrb
    ha_out, hb_out = away(ha, FAR), away(hb, NEAR)
    hra, hrb = swap(ha_out, FAR, n_dp), swap(hb_out, NEAR, n_dp)
    ob, hb_out = tie(ob, hb_out)
    ob_ = swap(ob, NEAR, n_dp)
    (ig,) = attn_bwd(False, 2, 1, *peer, (gm, part), ig, (ha_out, hb_out, ob))
    hra, hrb, i_, ig = tie(hra, hrb, i_, ig)
    h = jnp.concatenate([kept(ha, FAR) + hra, kept(hb, NEAR) + hrb])
    h_ = exchange(h, 2 * FAR, n_dp)
    i = in_order(FAR, i, i_)
    i_ = swap(i, NEAR, n_dp)
    (input_grad,) = attn_bwd(False, 3, 1, *peer, (gm, part), ig, (h, i))
    h_, input_grad = tie(h_, input_grad)
    h = beyond(h + h_, n_dp)
    rows = h.shape[0] // 2
    ha, hb = h[:rows], h[rows:]
    hra, hrb = swap(ha, FAR, n_dp), swap(hb, NEAR, n_dp)
    hra, hrb, i_, oa_, ob_ = tie(hra, hrb, i_, oa_, ob_)
    ha, hb = in_order(FAR, ha, hra), in_order(NEAR, hb, hrb)
    hra, hrb = swap(ha, NEAR, n_dp), swap(hb, FAR, n_dp)
    i = in_order(NEAR, i, i_)
    i_ = swap(i, CORE, n_dp)
    o = in_order(NEAR, o, jnp.concatenate([oa_, ob_]))
    o_ = swap(o, CORE, n_dp)
    owg = join(o, o_)
    hra, hrb, owg, i_ = tie(hra, hrb, owg, i_)
    ha, hb = in_order(NEAR, ha, hra), in_order(FAR, hb, hrb)
    hra, hrb = swap(ha, CORE, n_dp), swap(hb, CORE, n_dp)
    iwg = join(i, i_)
    hra, hrb, iwg = tie(hra, hrb, iwg)
    qwg, kwg, vwg, mwg, *vectors = finish(ha, hra, hb, hrb)
    qb, vb, mb, fg, fb, ib, ob, sg, sb = vectors
    return (
        layer_out, input_grad, qwg, kwg, vwg, qb, vb, mwg, mb, fg, fb, iwg, ib, owg, ob, sg, sb,
    )


def solution(mesh):
    col, row, rep = P(None, "tensor"), P("tensor", None), P()
    vec, tok = P("tensor"), P("dp", None)
    return jax.shard_map(
        partial(local, mesh.shape["dp"]),
        mesh=mesh,
        in_specs=(tok, col, col, col, vec, vec, row, rep, rep, rep, col, vec, row, rep, rep, rep, tok, tok),
        out_specs=(tok, tok, col, col, col, vec, vec, row, rep, rep, rep, col, vec, row, rep, rep, rep),
        check_vma=False,
    )
```

```python
import math
from functools import partial

import jax
import jax.numpy as jnp
from jax import lax
from jax.experimental import pallas as pl
from jax.experimental.pallas import tpu as pltpu
from jax.sharding import PartitionSpec as P

HD = 64
MAXLEN = 512
EPSILON = 1e-06
INV_SQRT2 = 1.0 / math.sqrt(2.0)
INV_SQRT_2PI = 1.0 / math.sqrt(2.0 * math.pi)
NEG = -1e30
FWD_GROUP = (1, 6, 6)
BWD_GROUP = (2, 6, 6)
BF = jnp.bfloat16
F32 = jnp.float32
PAD = 32
V_QV, V_MB, V_FG, V_FB, V_IB, V_OB, V_SG, V_SB = (0, 0), (0, 1), (1, 0), (1, 1), 2, (3, 0), (3, 1), (4, 0)


def vector(ref, place):
    row, side = place
    d = ref.shape[1] // 2
    return ref[row : row + 1, side * d : (side + 1) * d]


def dot(a, b):
    return lax.dot_general(a, b, (((1,), (0,)), ((), ())), preferred_element_type=F32)


def dot_bt(a, b):
    return lax.dot_general(a, b, (((1,), (1,)), ((), ())), preferred_element_type=F32)


def dot_at(a, b):
    return lax.dot_general(a, b, (((0,), (0,)), ((), ())), preferred_element_type=F32)


def core_halves(size):
    core = lax.axis_index("dp") & 1
    return [pl.ds(pl.multiple_of(side * size, 128), size) for side in (core, 1 - core)]


def head_lanes(rows):
    return lax.broadcasted_iota(jnp.int32, (rows, 2 * HD), 1) < HD


def params(mib):
    return pltpu.CompilerParams(vmem_limit_bytes=mib * 1024 * 1024)


def full(shape):
    return pl.BlockSpec(shape, lambda b: (0,) * len(shape), pipeline_mode=pl.Buffered(1))


def rows_spec(cols, start=0):
    return pl.BlockSpec((MAXLEN, cols), lambda b: (b + start, 0))


SMEM = pl.BlockSpec(memory_space=pltpu.SMEM)
ANY = pl.BlockSpec(memory_space=pl.ANY)


def cost(us):
    return pl.CostEstimate(flops=int(us * 1e9), bytes_accessed=1_000_000, transcendentals=0)


def attn_fwd_kernel(start, skip, len_ref, h_ref, wq_ref, wk_ref, wv_ref, vec_ref, *rest):
    q_ref, k_ref, v_ref, c_ref, l_ref = rest[skip:]
    half = wq_ref.shape[1]
    pairs = half // (2 * HD)
    b = pl.program_id(0) + start
    h = h_ref[...]
    q_ref[...] = (dot(h, wq_ref[...]) + vec_ref[0:1, :half]).astype(BF)
    k_ref[...] = dot(h, wk_ref[...]).astype(BF)
    v_ref[...] = (dot(h, wv_ref[...]) + vec_ref[0:1, half : 2 * half]).astype(BF)
    l_ref[...] = jnp.zeros_like(l_ref)
    for kind in range(3):

        @pl.when(lax.rem(b, 3) == kind)
        def _():
            span = MAXLEN >> kind
            low_lanes = head_lanes(span)
            lane = lax.broadcasted_iota(jnp.int32, (span, 128), 1)
            for seq in range(1 << kind):
                rows = slice(seq * span, (seq + 1) * span)
                live = lax.broadcasted_iota(jnp.int32, (1, span), 1) < len_ref[b, seq]
                bias = jnp.where(live, 0.0, NEG)
                logs = jnp.zeros((span, 128), F32)
                outs = []
                group = FWD_GROUP[kind]
                for first in range(0, 2 * pairs, group):
                    heads = range(first, first + group)
                    cols = [slice(head // 2 * 2 * HD, (head // 2 + 1) * 2 * HD) for head in heads]
                    qs = [
                        jnp.where(low_lanes if head % 2 == 0 else ~low_lanes, q_ref[rows, at] * BF(0.125), BF(0))
                        for head, at in zip(heads, cols)
                    ]
                    scores = [dot_bt(q, k_ref[rows, at]) + bias for q, at in zip(qs, cols)]
                    peaks = [jnp.max(x, axis=-1, keepdims=True) for x in scores]
                    exps = [jnp.exp(x - m) for x, m in zip(scores, peaks)]
                    totals = [jnp.sum(x, axis=-1, keepdims=True) for x in exps]
                    probs = [(x * (1.0 / z)).astype(BF) for x, z in zip(exps, totals)]
                    outs += [dot(p, v_ref[rows, at]) for p, at in zip(probs, cols)]
                    for head, m, z in zip(heads, peaks, totals):
                        logs = jnp.where(lane == head, m + jnp.log(z), logs)
                for pair in range(pairs):
                    both = jnp.where(low_lanes, outs[2 * pair], outs[2 * pair + 1])
                    c_ref[rows, pair * 2 * HD : (pair + 1) * 2 * HD] = both.astype(BF)
                l_ref[:, rows] = logs.T[:8]


def attn_fwd(lengths, hidden, wq, wk, wv, vec, start, count, prior=None, after=(), peer=False):
    n, d = hidden.shape
    half = wq.shape[1]
    blocks = n // MAXLEN
    wide = jax.ShapeDtypeStruct((n, half), BF)
    prior = list(prior or ())
    extra = prior + list(after)
    return pl.pallas_call(
        partial(attn_fwd_kernel, start, len(extra)),
        grid=(count,),
        in_specs=[
            SMEM, rows_spec(d, start), full((d, half)), full((d, half)), full((d, half)), full(vec.shape),
            *[ANY] * len(extra),
        ],
        out_specs=[rows_spec(half, start)] * 4 + [pl.BlockSpec((8, MAXLEN), lambda b: (b + start, 0))],
        out_shape=[wide] * 4 + [jax.ShapeDtypeStruct((8 * blocks, MAXLEN), F32)],
        input_output_aliases={6 + i: i for i in range(len(prior))},
        compiler_params=params(20 if peer else 60),
        cost_estimate=cost(7 * count),
        name="attn_fwd",
    )(lengths, hidden, wq, wk, wv, vec, *extra)


def live_column(len_ref, b):
    pos = lax.broadcasted_iota(jnp.int32, (MAXLEN, 1), 0)
    kind = lax.rem(b, 3)
    shift = 9 - kind
    seg = lax.shift_right_logical(pos, shift)
    off = pos - lax.shift_left(seg, shift)
    picked = jnp.full((MAXLEN, 1), len_ref[b, 0], jnp.int32)
    for slot in range(1, 4):
        picked = jnp.where(seg == slot, len_ref[b, slot], picked)
    return (off < picked).astype(F32)


def norm_stats(x):
    center = x - jnp.mean(x, axis=-1, keepdims=True)
    inverse = lax.rsqrt(jnp.mean(center * center, axis=-1, keepdims=True) + EPSILON)
    return center * inverse, inverse


def accumulate(ref, value, first_step):
    @pl.when(first_step)
    def _():
        ref[...] = value

    @pl.when(jnp.logical_not(first_step))
    def _():
        ref[...] += value


def ff_fwd_kernel(
    len_ref, h_ref, co_ref, cp_ref, cot_ref, wmo_ref, wmp_ref, wio_ref, wip_ref, woo_ref, wop_ref, vec_ref, pvec_ref,
    out_ref, x_ref, low_ref, gs_ref, lo_ref, gpo_ref, gpp_ref, owk_ref, owa_ref, sums_ref, act_ref, pa_ref, pb_ref,
):
    b = pl.program_id(0)
    d = h_ref.shape[1]
    ff = wio_ref.shape[1]
    width = 512
    pa_ref[...] = dot(co_ref[...], wmo_ref[...])
    pb_ref[...] = dot(cp_ref[...], wmp_ref[...])
    mixed = (pa_ref[...] + pb_ref[...]) + vector(vec_ref, V_MB)
    x = h_ref[...].astype(F32) + mixed
    x_ref[...] = x
    n1, _ = norm_stats(x)
    first = n1 * vector(vec_ref, V_FG) + vector(vec_ref, V_FB)
    low = first.astype(BF)
    low_ref[...] = low
    for wi, wo, vec, gp_ref, part_ref, keep in (
        (wio_ref, woo_ref, vec_ref, gpo_ref, pa_ref, True),
        (wip_ref, wop_ref, pvec_ref, gpp_ref, pb_ref, False),
    ):
        part = None
        for c in range(ff // width):
            cols = slice(c * width, (c + 1) * width)
            inner = dot(low, wi[:, cols]) + vec[V_IB : V_IB + 1, cols]
            cdf = 0.5 * (1.0 + lax.erf(inner * INV_SQRT2))
            gp_ref[:, cols] = cdf + inner * (jnp.exp(-0.5 * inner * inner) * INV_SQRT_2PI)
            active = (inner * cdf).astype(BF)
            if keep:
                act_ref[:, cols] = active
            term = dot(active, wo[cols, :])
            part = term if part is None else part + term
        part_ref[...] = part
    r = first + ((pa_ref[...] + pb_ref[...]) + vector(vec_ref, V_OB))
    n2, inv2 = norm_stats(r)
    gain = vector(vec_ref, V_SG)
    out_ref[...] = (n2 * gain + vector(vec_ref, V_SB)).astype(BF)
    g = cot_ref[...].astype(F32) * live_column(len_ref, b)
    scaled = g * gain
    gs = inv2 * (
        scaled - jnp.mean(scaled, axis=-1, keepdims=True) - n2 * jnp.mean(scaled * n2, axis=-1, keepdims=True)
    )
    gs_ref[...] = gs
    lo = gs.astype(BF)
    lo_ref[...] = lo
    sums = jnp.concatenate(
        [
            jnp.sum(gs, axis=0, keepdims=True),
            jnp.sum(g * n2, axis=0, keepdims=True),
            jnp.sum(g, axis=0, keepdims=True),
            jnp.zeros((5, d), F32),
        ],
        axis=0,
    )
    accumulate(sums_ref, sums, b == 0)
    for ref, cols in zip((owk_ref, owa_ref), core_halves(ff // 2)):
        accumulate(ref, dot_at(act_ref[:, cols], lo), b == 0)


def ff_fwd(lengths, hidden, co, cp, cot, wmo, wmp, wio, wip, woo, wop, vec, pvec):
    n, d = hidden.shape
    half = co.shape[1]
    ff = wio.shape[1]
    return pl.pallas_call(
        ff_fwd_kernel,
        grid=(n // MAXLEN,),
        in_specs=[
            SMEM, rows_spec(d), rows_spec(half), rows_spec(half), rows_spec(d), full((half, d)), full((half, d)),
            full((d, ff)), full((d, ff)), full((ff, d)), full((ff, d)), full(vec.shape), full(pvec.shape),
        ],
        out_specs=[
            rows_spec(d), rows_spec(d), rows_spec(d), rows_spec(d), rows_spec(d), rows_spec(ff), rows_spec(ff),
            full((ff // 2, d)), full((ff // 2, d)), full((8, d)),
        ],
        out_shape=[
            jax.ShapeDtypeStruct((n, d), BF),
            jax.ShapeDtypeStruct((n, d), F32),
            jax.ShapeDtypeStruct((n, d), BF),
            jax.ShapeDtypeStruct((n, d), F32),
            jax.ShapeDtypeStruct((n, d), BF),
            jax.ShapeDtypeStruct((n, ff), F32),
            jax.ShapeDtypeStruct((n, ff), F32),
            jax.ShapeDtypeStruct((ff // 2, d), F32),
            jax.ShapeDtypeStruct((ff // 2, d), F32),
            jax.ShapeDtypeStruct((8, d), F32),
        ],
        scratch_shapes=[pltpu.VMEM((MAXLEN, ff), BF), pltpu.VMEM((MAXLEN, d), F32), pltpu.VMEM((MAXLEN, d), F32)],
        compiler_params=params(46),
        cost_estimate=cost(58),
        name="ff_fwd",
    )(lengths, hidden, co, cp, cot, wmo, wmp, wio, wip, woo, wop, vec, pvec)


def ff_bwd_half(lo, wi_ref, wo_ref, gp_ref, gi_ref, part_ref):
    width = 512
    part = None
    for c in range(wi_ref.shape[1] // width):
        cols = slice(c * width, (c + 1) * width)
        gi = (dot_bt(lo, wo_ref[cols, :]) * gp_ref[:, cols]).astype(BF)
        if gi_ref is not None:
            gi_ref[:, cols] = gi
        term = dot_bt(gi, wi_ref[:, cols])
        part = term if part is None else part + term
    part_ref[...] = part


def ff_bwd_own_kernel(skip, lo_ref, low_ref, gp_ref, wi_ref, wo_ref, *rest):
    part_ref, iwk_ref, iwa_ref, isum_ref, gi_ref = rest[skip:]
    b = pl.program_id(0)
    ff_bwd_half(lo_ref[...], wi_ref, wo_ref, gp_ref, gi_ref, part_ref)
    gi = gi_ref[...]
    for ref, cols in zip((iwk_ref, iwa_ref), core_halves(low_ref.shape[1] // 2)):
        accumulate(ref, dot_at(low_ref[:, cols], gi), b == 0)
    accumulate(isum_ref, jnp.sum(gi.astype(F32), axis=0, keepdims=True), b == 0)


def ff_bwd_own(lo, low, gp, wi, wo, *after):
    n, d = lo.shape
    ff = wi.shape[1]
    return pl.pallas_call(
        partial(ff_bwd_own_kernel, len(after)),
        grid=(n // MAXLEN,),
        in_specs=[rows_spec(d), rows_spec(d), rows_spec(ff), full((d, ff)), full((ff, d)), *[ANY] * len(after)],
        out_specs=[rows_spec(d), full((d // 2, ff)), full((d // 2, ff)), full((1, ff))],
        out_shape=[
            jax.ShapeDtypeStruct((n, d), F32),
            jax.ShapeDtypeStruct((d // 2, ff), F32),
            jax.ShapeDtypeStruct((d // 2, ff), F32),
            jax.ShapeDtypeStruct((1, ff), F32),
        ],
        scratch_shapes=[pltpu.VMEM((MAXLEN, ff), BF)],
        compiler_params=params(30),
        cost_estimate=cost(26),
        name="ff_bwd_own",
    )(lo, low, gp, wi, wo, *after)


def ff_bwd_peer_kernel(
    skip, lo_ref, gs_ref, x_ref, gp_ref, opart_ref, co_ref, wi_ref, wo_ref, vec_ref, *rest
):
    gm_ref, lm_ref, mwg_ref, sums_ref, part_ref = rest[skip:]
    b = pl.program_id(0)
    d = lo_ref.shape[1]
    ff_bwd_half(lo_ref[...], wi_ref, wo_ref, gp_ref, None, part_ref)
    g = gs_ref[...] + (opart_ref[...] + part_ref[...])
    n1, inv1 = norm_stats(x_ref[...])
    scaled = g * vector(vec_ref, V_FG)
    gm = inv1 * (
        scaled - jnp.mean(scaled, axis=-1, keepdims=True) - n1 * jnp.mean(scaled * n1, axis=-1, keepdims=True)
    )
    gm_ref[...] = gm
    lm = gm.astype(BF)
    lm_ref[...] = lm
    sums = jnp.concatenate(
        [
            jnp.sum(gm, axis=0, keepdims=True),
            jnp.sum(g * n1, axis=0, keepdims=True),
            jnp.sum(g, axis=0, keepdims=True),
            jnp.zeros((5, d), F32),
        ],
        axis=0,
    )
    accumulate(sums_ref, sums, b == 0)
    accumulate(mwg_ref, dot_at(co_ref[...], lm), b == 0)


def ff_bwd_peer(lo, gs, x, gp, opart, co, wi, wo, vec, *after):
    n, d = lo.shape
    half = co.shape[1]
    ff = wi.shape[1]
    return pl.pallas_call(
        partial(ff_bwd_peer_kernel, len(after)),
        grid=(n // MAXLEN,),
        in_specs=[
            rows_spec(d), rows_spec(d), rows_spec(d), rows_spec(ff), rows_spec(d), rows_spec(half), full((d, ff)),
            full((ff, d)), full(vec.shape), *[ANY] * len(after),
        ],
        out_specs=[rows_spec(d), rows_spec(d), full((half, d)), full((8, d))],
        out_shape=[
            jax.ShapeDtypeStruct((n, d), F32),
            jax.ShapeDtypeStruct((n, d), BF),
            jax.ShapeDtypeStruct((half, d), F32),
            jax.ShapeDtypeStruct((8, d), F32),
        ],
        scratch_shapes=[pltpu.VMEM((MAXLEN, d), F32)],
        compiler_params=params(30),
        cost_estimate=cost(25),
        name="ff_bwd_peer",
    )(lo, gs, x, gp, opart, co, wi, wo, vec, *after)


def attn_bwd_kernel(own, start, skip, len_ref, lm_ref, wm_ref, q_ref, k_ref, v_ref, l_ref, wq_ref, wk_ref, wv_ref, *rest):
    if own:
        given = 3 if start else 5
        h_ref, *given = rest[:given]
        part_ref, wk_out, wa_out, gc_ref, dq_ref, dk_ref, dv_ref = rest[len(given) + 1 + skip :]
    else:
        gm_ref, opart_ref = rest[:2]
        ig_ref, gc_ref, dq_ref, dk_ref, dv_ref, part_ref = rest[2 + skip :]
    half = wq_ref.shape[1]
    pairs = half // (2 * HD)
    b = pl.program_id(0) + start
    gc_ref[...] = dot_bt(lm_ref[...], wm_ref[...]).astype(BF)
    for kind in range(3):

        @pl.when(lax.rem(b, 3) == kind)
        def _():
            span = MAXLEN >> kind
            low_lanes = head_lanes(span)
            for seq in range(1 << kind):
                rows = slice(seq * span, (seq + 1) * span)
                live = lax.broadcasted_iota(jnp.int32, (span, 1), 0) < len_ref[b, seq]
                bias = jnp.where(live, 0.0, NEG)
                dqs, dks, dvs = [], [], []
                group = BWD_GROUP[kind]
                for first in range(0, 2 * pairs, group):
                    heads = range(first, first + group)
                    cols = [slice(head // 2 * 2 * HD, (head // 2 + 1) * 2 * HD) for head in heads]
                    masks = [low_lanes if head % 2 == 0 else ~low_lanes for head in heads]
                    qs = [q_ref[rows, at] * BF(0.125) for at in cols]
                    ups = [gc_ref[rows, at] for at in cols]
                    scores = [
                        dot_bt(k_ref[rows, at], jnp.where(mask, q, BF(0))) + bias for q, at, mask in zip(qs, cols, masks)
                    ]
                    dprobs = [
                        dot_bt(v_ref[rows, at], jnp.where(mask, up, BF(0))) for up, at, mask in zip(ups, cols, masks)
                    ]
                    probs = [jnp.exp(x - l_ref[head : head + 1, rows]) for x, head in zip(scores, heads)]
                    deltas = [jnp.sum(p * dp, axis=0, keepdims=True) for p, dp in zip(probs, dprobs)]
                    dscores = [(p * (dp - delta)).astype(BF) for p, dp, delta in zip(probs, dprobs, deltas)]
                    dvs += [dot(p.astype(BF), up) for p, up in zip(probs, ups)]
                    dks += [dot(ds, q) for ds, q in zip(dscores, qs)]
                    dqs += [dot_at(ds, k_ref[rows, at]) for ds, at in zip(dscores, cols)]
                for pair in range(pairs):
                    at = slice(pair * 2 * HD, (pair + 1) * 2 * HD)
                    dv_ref[rows, at] = jnp.where(low_lanes, dvs[2 * pair], dvs[2 * pair + 1]).astype(BF)
                    dk_ref[rows, at] = jnp.where(low_lanes, dks[2 * pair], dks[2 * pair + 1]).astype(BF)
                    dq = jnp.where(low_lanes, dqs[2 * pair], dqs[2 * pair + 1]) * 0.125
                    dq_ref[rows, at] = dq.astype(BF)

    dq, dk, dv = dq_ref[...], dk_ref[...], dv_ref[...]
    part = (dot_bt(dq, wq_ref[...]) + dot_bt(dk, wk_ref[...])) + dot_bt(dv, wv_ref[...])
    part_ref[...] = part
    if own:
        d = h_ref.shape[1]
        sums = jnp.concatenate(
            [jnp.sum(dq.astype(F32), axis=0, keepdims=True), jnp.sum(dv.astype(F32), axis=0, keepdims=True)], axis=1
        )
        first_step = b == start
        core = lax.axis_index("dp") & 1
        for side, (out, cols) in enumerate(zip((wk_out, wa_out), core_halves(half))):
            holds = (core == side).astype(F32)

            @pl.when(first_step)
            def _(side=side, out=out, cols=cols, holds=holds):
                if start:
                    out[...] = given[side][...]
                    return
                mwg_ref, fsum_ref, isum_ref, osum_ref = given
                pad = jnp.zeros((1, d), F32)
                top = jnp.concatenate([pad, fsum_ref[0:1, :]], axis=1)
                mid = jnp.concatenate([fsum_ref[1:2, :], fsum_ref[2:3, :]], axis=1)
                low = jnp.concatenate([osum_ref[0:1, :], osum_ref[1:2, :]], axis=1)
                end = jnp.concatenate([osum_ref[2:3, :], pad], axis=1)
                vectors = jnp.concatenate([top, mid, isum_ref[...], low, end, jnp.zeros((3, 2 * d), F32)], axis=0)
                out[:half, : 3 * half] = jnp.zeros((half, 3 * half), F32)
                out[:half, 3 * half :] = mwg_ref[:, cols]
                out[half : half + 8, :] = vectors * holds
                out[half + 8 :, :] = jnp.zeros((PAD - 8, 2 * d), F32)

            h = h_ref[:, cols]
            for i, grad in enumerate((dq, dk, dv)):
                out[:half, i * half : (i + 1) * half] += dot_at(h, grad)
            out[half : half + 1, :d] += sums * holds
    else:
        ig_ref[...] = (gm_ref[...] + (opart_ref[...] + part_ref[...])).astype(BF)


def attn_bwd(own, start, count, lengths, lm, wm, q, k, v, logs, wq, wk, wv, extra, prior=None, after=()):
    n, d = lm.shape
    half = wq.shape[1]
    after = ([] if prior is None else [prior]) + list(after)
    if own:
        extra_specs = [rows_spec(d, start)] + [full(x.shape) for x in extra[1:]]
        out_specs = [rows_spec(d, start)] + [full((half + PAD, 4 * half))] * 2
        out_shape = [jax.ShapeDtypeStruct((n, d), F32)] + [jax.ShapeDtypeStruct((half + PAD, 4 * half), F32)] * 2
    else:
        extra_specs = [rows_spec(d, start)] * 2
        out_specs = [rows_spec(d, start)]
        out_shape = [jax.ShapeDtypeStruct((n, d), BF)]
    return pl.pallas_call(
        partial(attn_bwd_kernel, own, start, len(after)),
        grid=(count,),
        in_specs=[
            SMEM, rows_spec(d, start), full((half, d)), rows_spec(half, start), rows_spec(half, start),
            rows_spec(half, start), pl.BlockSpec((8, MAXLEN), lambda b: (b + start, 0)), full((d, half)),
            full((d, half)), full((d, half)), *extra_specs, *[ANY] * len(after),
        ],
        out_specs=out_specs,
        out_shape=out_shape,
        input_output_aliases={} if prior is None else {10 + len(extra): 0},
        scratch_shapes=[pltpu.VMEM((MAXLEN, half), BF)] * 4 + ([] if own else [pltpu.VMEM((MAXLEN, d), F32)]),
        compiler_params=params(26 if own else 60),
        cost_estimate=cost(12 * count if own else 40),
        name="attn_bwd_own" if own else "attn_bwd_peer",
    )(lengths, lm, wm, q, k, v, logs, wq, wk, wv, *extra, *after)


CORE, NEAR, FAR = 1, 2, 4
TENSOR_SWAP = [(0, 1), (1, 0)]


def bit_of(mask):
    return (lax.axis_index("dp") & mask) != 0


def swap(x, mask, n_dp):
    return lax.ppermute(x, "dp", [(i, i ^ mask) for i in range(n_dp)])


def in_order(mask, mine, other):
    return jnp.where(bit_of(mask), jnp.concatenate([other, mine]), jnp.concatenate([mine, other]))


def away(x, mask):
    rows = x.shape[0] // 2
    return lax.dynamic_slice_in_dim(x, jnp.where(bit_of(mask), 0, rows), rows, 0)


def kept(x, mask):
    rows = x.shape[0] // 2
    return lax.dynamic_slice_in_dim(x, jnp.where(bit_of(mask), rows, 0), rows, 0)


def exchange(x, mask, n_dp):
    return swap(x, mask, n_dp) if mask < n_dp else jnp.zeros_like(x)


def join_kernel(mine_ref, other_ref, out_ref):
    rows = mine_ref.shape[0]
    core = lax.axis_index("dp") & 1
    out_ref[pl.ds(pl.multiple_of(core * rows, 8), rows), :] = mine_ref[...]
    out_ref[pl.ds(pl.multiple_of((1 - core) * rows, 8), rows), :] = other_ref[...]


def join(mine, other):
    return pl.pallas_call(
        join_kernel,
        out_shape=jax.ShapeDtypeStruct((2 * mine.shape[0], mine.shape[1]), mine.dtype),
        compiler_params=params(20),
        cost_estimate=cost(0.1),
        name="join",
    )(mine, other)


def beyond(x, n_dp):
    mask = 4 * FAR
    while mask < n_dp:
        x = x + swap(x, mask, n_dp)
        mask *= 2
    return x


def piece(arrays, masks, base, rows):
    index = jnp.int32(0)
    for mask in masks:
        index = index * 2 + bit_of(mask).astype(jnp.int32)
    cut = [lax.dynamic_slice_in_dim(a, base + index * rows, rows, 0) for a in arrays]
    return jnp.concatenate(cut, axis=1).astype(F32)


def tie(*arrays):
    return lax.optimization_barrier(arrays)


def prepare_kernel(*refs):
    weights, vectors, (vec_ref, out_ref) = refs[:4], refs[4:-2], refs[-2:]
    d = vec_ref.shape[1] // 2
    qb, vb, mb, fg, fb, ib, ob, sg, sb = [ref[...].astype(F32).reshape(1, -1) for ref in vectors]
    zero = jnp.zeros((1, d), F32)
    rows = [(qb, vb, mb), (fg, fb), (ib,), (ob, sg), (sb, zero)]
    vec = jnp.concatenate(
        [jnp.concatenate(row, axis=1) for row in rows] + [jnp.zeros((3, 2 * d), F32)], axis=0
    )
    vec_ref[...] = vec
    me = lax.axis_index("dp")
    core, near, far = me & 1, (me >> 1) & 1, (me >> 2) & 1
    half = d // 2
    rows = d // 16
    for base, index in ((0, core * 4 + far * 2 + near), (8 * rows, core * 4 + near * 2 + far)):
        at = pl.ds(pl.multiple_of(base + index * rows, 16), rows)
        to = slice(base // 8, base // 8 + rows)
        for i in range(3):
            out_ref[to, i * half : (i + 1) * half] = weights[i][at, :].astype(F32)
        at = pl.ds(pl.multiple_of(index * rows, 16), rows)
        cols = slice(0, half) if base == 0 else slice(half, d)
        out_ref[to, 3 * half :] = weights[3][at, cols].astype(F32)
    out_ref[2 * rows :, :] = vec


def prepare(weights, vectors):
    d = weights[0].shape[0]
    return pl.pallas_call(
        prepare_kernel,
        out_shape=[jax.ShapeDtypeStruct((8, 2 * d), F32), jax.ShapeDtypeStruct((d // 8 + 8, 2 * d), F32)],
        compiler_params=params(60),
        cost_estimate=cost(2),
        name="prepare",
    )(*weights, *vectors)


def finish_kernel(a_ref, ra_ref, b_ref, rb_ref, q_ref, k_ref, v_ref, m_ref, *vectors):
    half = m_ref.shape[0]
    d = 2 * half
    mine, other = core_halves(half)
    core = lax.axis_index("dp") & 1
    for cols, x_ref, y_ref in ((mine, a_ref, b_ref), (other, ra_ref, rb_ref)):
        q_ref[cols, :] = x_ref[:half, :half]
        k_ref[cols, :] = x_ref[:half, half:]
        v_ref[cols, :] = y_ref[:half, :half]
        m_ref[:, cols] = y_ref[:half, half:]
    pad = slice(half, half + 8)
    left = jnp.where(core == 0, a_ref[pad, :], ra_ref[pad, :])
    right = jnp.where(core == 0, b_ref[pad, :], rb_ref[pad, :])
    rows = (
        left[0:1, :half], left[0:1, half:], right[0:1], left[1:2], right[1:2],
        jnp.concatenate([left[2:3], right[2:3]], axis=1), left[3:4], right[3:4], left[4:5],
    )
    for ref, row in zip(vectors, rows):
        ref[...] = row.reshape(-1)


def finish(a, ra, b, rb):
    d = a.shape[1]
    half = d // 2
    return pl.pallas_call(
        finish_kernel,
        out_shape=[jax.ShapeDtypeStruct((d, half), F32)] * 3
        + [jax.ShapeDtypeStruct((half, d), F32)]
        + [jax.ShapeDtypeStruct((size,), F32) for size in (half, half, d, d, d, 2 * d, d, d, d)],
        compiler_params=params(20),
        cost_estimate=cost(0.1),
        name="finish",
    )(a, ra, b, rb)


def assemble_kernel(square, a_ref, ra_ref, b_ref, rb_ref, *outs):
    rows = a_ref.shape[0]
    odd = lax.axis_index("dp") & CORE
    for base, mine, other in ((0, a_ref, ra_ref), (2 * rows, b_ref, rb_ref)):
        for ref, side in ((mine, odd), (other, 1 - odd)):
            at = pl.ds(pl.multiple_of(base + side * rows, 16), rows)
            if not square:
                outs[0][at, :] = ref[...].astype(BF)
                continue
            half = ref.shape[1] // 4
            for i in range(3):
                outs[i][at, :] = ref[:, i * half : (i + 1) * half].astype(BF)
            at = pl.ds(pl.multiple_of(side * rows, 16), rows)
            left = base == 0
            cols = slice(0, half) if left else slice(half, 2 * half)
            outs[3][at, cols] = ref[:, 3 * half :].astype(BF)


def assemble(square, a, ra, b, rb):
    rows, cols = 4 * a.shape[0], a.shape[1]
    half = cols // 4
    if square:
        shapes = [(rows, half)] * 3 + [(rows // 2, 2 * half)]
    else:
        shapes = [(rows, cols)]
    return pl.pallas_call(
        partial(assemble_kernel, square),
        out_shape=[jax.ShapeDtypeStruct(shape, BF) for shape in shapes],
        compiler_params=params(16),
        cost_estimate=cost(4),
        name="assemble",
    )(a, ra, b, rb)


def local(
    n_dp, hidden_in, query_weight, key_weight, value_weight, query_bias, value_bias, mixer_weight, mixer_bias,
    first_gain, first_bias, inner_weight, inner_bias, outer_weight, outer_bias, second_gain, second_bias, lengths,
    cotangent,
):
    n, d = hidden_in.shape
    half = query_weight.shape[1]
    ff = inner_weight.shape[1]
    vec, h_out = prepare(
        (query_weight, key_weight, value_weight, mixer_weight),
        (
            query_bias, value_bias, mixer_bias, first_gain, first_bias, inner_bias, outer_bias, second_gain,
            second_bias,
        ),
    )
    sixteenth = d // 16
    i_out = jnp.concatenate(
        [
            piece([inner_weight], (CORE, FAR, NEAR), 0, sixteenth),
            piece([inner_weight], (CORE, NEAR, FAR), d // 2, sixteenth),
        ]
    )
    eighth = ff // 8
    o_out = jnp.concatenate(
        [piece([outer_weight], (CORE, NEAR), 0, eighth), piece([outer_weight], (CORE, FAR), ff // 2, eighth)]
    )
    h0 = lax.ppermute(h_out, "tensor", TENSOR_SWAP)
    own = list(attn_fwd(lengths, hidden_in, query_weight, key_weight, value_weight, vec, 0, 2))
    h0, i_out, own[0] = tie(h0, i_out, own[0])
    i0 = lax.ppermute(i_out, "tensor", TENSOR_SWAP)
    ha, hb, pvec = h0[:sixteenth], h0[sixteenth : 2 * sixteenth], h0[2 * sixteenth :]
    hra, hrb = swap(ha, NEAR, n_dp), swap(hb, FAR, n_dp)
    qo, ko, vo, co, lgo = attn_fwd(
        lengths, hidden_in, query_weight, key_weight, value_weight, vec, 2, 2, own, (ha, hb)
    )
    hra, hrb, i0, co, o_out = tie(hra, hrb, i0, co, o_out)
    ha, hb = in_order(NEAR, ha, hra), in_order(FAR, hb, hrb)
    hra, hrb = swap(ha, FAR, n_dp), swap(hb, NEAR, n_dp)
    o0 = lax.ppermute(o_out, "tensor", TENSOR_SWAP)
    ia, ib = i0[:sixteenth], i0[sixteenth:]
    ira, irb = swap(ia, NEAR, n_dp), swap(ib, FAR, n_dp)
    ha, hb = in_order(FAR, ha, hra), in_order(NEAR, hb, hrb)
    hra, hrb = swap(ha, CORE, n_dp), swap(hb, CORE, n_dp)
    ha, hb, ira, irb = tie(ha, hb, ira, irb)
    ia, ib = in_order(NEAR, ia, ira), in_order(FAR, ib, irb)
    ira, irb = swap(ia, FAR, n_dp), swap(ib, NEAR, n_dp)
    wqp, wkp, wvp, wmp = assemble(True, ha, hra, hb, hrb)
    peer = list(attn_fwd(lengths, hidden_in, wqp, wkp, wvp, pvec, 0, 2, None, (ia, ib), True))
    ira, irb, o0, peer[0] = tie(ira, irb, o0, peer[0])
    ia, ib = in_order(FAR, ia, ira), in_order(NEAR, ib, irb)
    ira, irb = swap(ia, CORE, n_dp), swap(ib, CORE, n_dp)
    oa, ob = o0[:eighth], o0[eighth:]
    ora, orb = swap(oa, NEAR, n_dp), swap(ob, FAR, n_dp)
    qp, kp, vp, cp, lgp = attn_fwd(lengths, hidden_in, wqp, wkp, wvp, pvec, 2, 2, peer, (ia, ib, oa, ob), True)
    ora, orb, cp = tie(ora, orb, cp)
    oa, ob = in_order(NEAR, oa, ora), in_order(FAR, ob, orb)
    ora, orb = swap(oa, CORE, n_dp), swap(ob, CORE, n_dp)
    (wip,) = assemble(False, ia, ira, ib, irb)
    (wop,) = assemble(False, oa, ora, ob, orb)
    layer_out, x, low, gs, lo, gpo, gpp, owk, owa, osums = ff_fwd(
        lengths, hidden_in, co, cp, cotangent, mixer_weight, wmp, inner_weight, wip, outer_weight, wop, vec, pvec
    )
    o, lo = tie(swap(owa, CORE, n_dp), lo)
    o1 = owk + o
    o_out = away(o1, NEAR)
    o = swap(o_out, NEAR, n_dp)
    opart, iwk, iwa, ibg = ff_bwd_own(lo, low, gpo, inner_weight, outer_weight, o_out)
    o, opart, iwa = tie(o, opart, iwa)
    i, opart = tie(swap(iwa, CORE, n_dp), opart)
    i1 = iwk + i
    i_out = away(i1, NEAR)
    i = swap(i_out, NEAR, n_dp)
    o2 = kept(o1, NEAR) + o
    o_out = away(o2, FAR)
    o = swap(o_out, FAR, n_dp)
    gm, lm, mwg, isums = ff_bwd_peer(lo, gs, x, gpp, opart, co, wip, wop, vec, o_out, i_out)
    o, i, lm = tie(o, i, lm)
    i2 = kept(i1, NEAR) + i
    i_out = away(i2, FAR)
    i = swap(i_out, FAR, n_dp)
    o3 = kept(o2, FAR) + o
    o3, i_out = tie(o3, i_out)
    o = exchange(o3, 2 * FAR, n_dp)
    own = (lengths, lm, mixer_weight, qo, ko, vo, lgo, query_weight, key_weight, value_weight)
    part, hk, ha = attn_bwd(True, 0, 2, *own, (hidden_in, mwg, isums, ibg, osums), None, (o3, i_out))
    o, i, part = tie(o, i, part)
    o = beyond(o3 + o, n_dp)
    o_ = swap(o, FAR, n_dp)
    i3 = kept(i2, FAR) + i
    i3, o = tie(i3, o)
    i = exchange(i3, 2 * FAR, n_dp)
    part, hk, ha = attn_bwd(True, 2, 2, *own, (hidden_in, hk, ha), part, (o, i3))
    h = swap(ha, CORE, n_dp)
    o_, ha = tie(o_, ha)
    o = in_order(FAR, o, o_)
    cut = o.shape[0] // 2
    oa_, ob = swap(o[:cut], NEAR, n_dp), o[cut:]
    peer = (lengths, lm, wmp, qp, kp, vp, lgp, wqp, wkp, wvp)
    (ig,) = attn_bwd(False, 0, 1, *peer, (gm, part), None, (o,))
    h, i, ig = tie(h, i, ig)
    h1 = hk + h
    ha, hb = h1[:, :d], h1[:, d:]
    ha_out, hb_out = away(ha, NEAR), away(hb, FAR)
    hra, hrb = swap(ha_out, NEAR, n_dp), swap(hb_out, FAR, n_dp)
    i = beyond(i3 + i, n_dp)
    i, hb_out = tie(i, hb_out)
    i_ = swap(i, FAR, n_dp)
    (ig,) = attn_bwd(False, 1, 1, *peer, (gm, part), ig, (ha_out, hb_out, i))
    hra, hrb, ob, ig = tie(hra, hrb, ob, ig)
    ha, hb = kept(ha, NEAR) + hra, kept(hb, FAR) + hrb
    ha_out, hb_out = away(ha, FAR), away(hb, NEAR)
    hra, hrb = swap(ha_out, FAR, n_dp), swap(hb_out, NEAR, n_dp)
    ob, hb_out = tie(ob, hb_out)
    ob_ = swap(ob, NEAR, n_dp)
    (ig,) = attn_bwd(False, 2, 1, *peer, (gm, part), ig, (ha_out, hb_out, ob))
    hra, hrb, i_, ig = tie(hra, hrb, i_, ig)
    h = jnp.concatenate([kept(ha, FAR) + hra, kept(hb, NEAR) + hrb])
    h_ = exchange(h, 2 * FAR, n_dp)
    i = in_order(FAR, i, i_)
    i_ = swap(i, NEAR, n_dp)
    (input_grad,) = attn_bwd(False, 3, 1, *peer, (gm, part), ig, (h, i))
    h_, input_grad = tie(h_, input_grad)
    h = beyond(h + h_, n_dp)
    rows = h.shape[0] // 2
    ha, hb = h[:rows], h[rows:]
    hra, hrb = swap(ha, FAR, n_dp), swap(hb, NEAR, n_dp)
    hra, hrb, i_, oa_, ob_ = tie(hra, hrb, i_, oa_, ob_)
    ha, hb = in_order(FAR, ha, hra), in_order(NEAR, hb, hrb)
    hra, hrb = swap(ha, NEAR, n_dp), swap(hb, FAR, n_dp)
    i = in_order(NEAR, i, i_)
    i_ = swap(i, CORE, n_dp)
    o = in_order(NEAR, o, jnp.concatenate([oa_, ob_]))
    o_ = swap(o, CORE, n_dp)
    owg = join(o, o_)
    hra, hrb, owg, i_ = tie(hra, hrb, owg, i_)
    ha, hb = in_order(NEAR, ha, hra), in_order(FAR, hb, hrb)
    hra, hrb = swap(ha, CORE, n_dp), swap(hb, CORE, n_dp)
    iwg = join(i, i_)
    hra, hrb, iwg = tie(hra, hrb, iwg)
    qwg, kwg, vwg, mwg, *vectors = finish(ha, hra, hb, hrb)
    qb, vb, mb, fg, fb, ib, ob, sg, sb = vectors
    return (
        layer_out, input_grad, qwg, kwg, vwg, qb, vb, mwg, mb, fg, fb, iwg, ib, owg, ob, sg, sb,
    )


def solution(mesh):
    col, row, rep = P(None, "tensor"), P("tensor", None), P()
    vec, tok = P("tensor"), P("dp", None)
    return jax.shard_map(
        partial(local, mesh.shape["dp"]),
        mesh=mesh,
        in_specs=(tok, col, col, col, vec, vec, row, rep, rep, rep, col, vec, row, rep, rep, rep, tok, tok),
        out_specs=(tok, tok, col, col, col, vec, vec, row, rep, rep, rep, col, vec, row, rep, rep, rep),
        check_vma=False,
    )
```

```python
import math
from functools import partial

import jax
import jax.numpy as jnp
from jax import lax
from jax.experimental import pallas as pl
from jax.experimental.pallas import tpu as pltpu
from jax.sharding import PartitionSpec as P

HD = 64
MAXLEN = 512
EPSILON = 1e-06
INV_SQRT2 = 1.0 / math.sqrt(2.0)
INV_SQRT_2PI = 1.0 / math.sqrt(2.0 * math.pi)
NEG = -1e30
FWD_GROUP = (1, 6, 6)
BWD_GROUP = (2, 6, 6)
BF = jnp.bfloat16
F32 = jnp.float32
PAD = 32
V_QV, V_MB, V_FG, V_FB, V_IB, V_OB, V_SG, V_SB = (0, 0), (0, 1), (1, 0), (1, 1), 2, (3, 0), (3, 1), (4, 0)


def vector(ref, place):
    row, side = place
    d = ref.shape[1] // 2
    return ref[row : row + 1, side * d : (side + 1) * d]


def dot(a, b):
    return lax.dot_general(a, b, (((1,), (0,)), ((), ())), preferred_element_type=F32)


def dot_bt(a, b):
    return lax.dot_general(a, b, (((1,), (1,)), ((), ())), preferred_element_type=F32)


def dot_at(a, b):
    return lax.dot_general(a, b, (((0,), (0,)), ((), ())), preferred_element_type=F32)


def core_halves(size):
    core = lax.axis_index("dp") & 1
    return [pl.ds(pl.multiple_of(side * size, 128), size) for side in (core, 1 - core)]


def head_lanes(rows):
    return lax.broadcasted_iota(jnp.int32, (rows, 2 * HD), 1) < HD


def params(mib):
    return pltpu.CompilerParams(vmem_limit_bytes=mib * 1024 * 1024)


def full(shape):
    return pl.BlockSpec(shape, lambda b: (0,) * len(shape), pipeline_mode=pl.Buffered(1))


def rows_spec(cols, start=0):
    return pl.BlockSpec((MAXLEN, cols), lambda b: (b + start, 0))


SMEM = pl.BlockSpec(memory_space=pltpu.SMEM)
ANY = pl.BlockSpec(memory_space=pl.ANY)


def cost(us):
    return pl.CostEstimate(flops=int(us * 1e9), bytes_accessed=1_000_000, transcendentals=0)


def attn_fwd_kernel(start, skip, len_ref, h_ref, wq_ref, wk_ref, wv_ref, vec_ref, *rest):
    q_ref, k_ref, v_ref, c_ref, l_ref = rest[skip:]
    half = wq_ref.shape[1]
    pairs = half // (2 * HD)
    b = pl.program_id(0) + start
    h = h_ref[...]
    q_ref[...] = (dot(h, wq_ref[...]) + vec_ref[0:1, :half]).astype(BF)
    k_ref[...] = dot(h, wk_ref[...]).astype(BF)
    v_ref[...] = (dot(h, wv_ref[...]) + vec_ref[0:1, half : 2 * half]).astype(BF)
    l_ref[...] = jnp.zeros_like(l_ref)
    for kind in range(3):

        @pl.when(lax.rem(b, 3) == kind)
        def _():
            span = MAXLEN >> kind
            low_lanes = head_lanes(span)
            lane = lax.broadcasted_iota(jnp.int32, (span, 128), 1)
            for seq in range(1 << kind):
                rows = slice(seq * span, (seq + 1) * span)
                live = lax.broadcasted_iota(jnp.int32, (1, span), 1) < len_ref[b, seq]
                bias = jnp.where(live, 0.0, NEG)
                logs = jnp.zeros((span, 128), F32)
                outs = []
                group = FWD_GROUP[kind]
                for first in range(0, 2 * pairs, group):
                    heads = range(first, first + group)
                    cols = [slice(head // 2 * 2 * HD, (head // 2 + 1) * 2 * HD) for head in heads]
                    qs = [
                        jnp.where(low_lanes if head % 2 == 0 else ~low_lanes, q_ref[rows, at] * BF(0.125), BF(0))
                        for head, at in zip(heads, cols)
                    ]
                    scores = [dot_bt(q, k_ref[rows, at]) + bias for q, at in zip(qs, cols)]
                    peaks = [jnp.max(x, axis=-1, keepdims=True) for x in scores]
                    exps = [jnp.exp(x - m) for x, m in zip(scores, peaks)]
                    totals = [jnp.sum(x, axis=-1, keepdims=True) for x in exps]
                    probs = [(x * (1.0 / z)).astype(BF) for x, z in zip(exps, totals)]
                    outs += [dot(p, v_ref[rows, at]) for p, at in zip(probs, cols)]
                    for head, m, z in zip(heads, peaks, totals):
                        logs = jnp.where(lane == head, m + jnp.log(z), logs)
                for pair in range(pairs):
                    both = jnp.where(low_lanes, outs[2 * pair], outs[2 * pair + 1])
                    c_ref[rows, pair * 2 * HD : (pair + 1) * 2 * HD] = both.astype(BF)
                l_ref[:, rows] = logs.T[:8]


def attn_fwd(lengths, hidden, wq, wk, wv, vec, start, count, prior=None, after=(), peer=False):
    n, d = hidden.shape
    half = wq.shape[1]
    blocks = n // MAXLEN
    wide = jax.ShapeDtypeStruct((n, half), BF)
    prior = list(prior or ())
    extra = prior + list(after)
    return pl.pallas_call(
        partial(attn_fwd_kernel, start, len(extra)),
        grid=(count,),
        in_specs=[
            SMEM, rows_spec(d, start), full((d, half)), full((d, half)), full((d, half)), full(vec.shape),
            *[ANY] * len(extra),
        ],
        out_specs=[rows_spec(half, start)] * 4 + [pl.BlockSpec((8, MAXLEN), lambda b: (b + start, 0))],
        out_shape=[wide] * 4 + [jax.ShapeDtypeStruct((8 * blocks, MAXLEN), F32)],
        input_output_aliases={6 + i: i for i in range(len(prior))},
        compiler_params=params(20 if peer else 60),
        cost_estimate=cost(7 * count),
        name="attn_fwd",
    )(lengths, hidden, wq, wk, wv, vec, *extra)


def live_column(len_ref, b):
    pos = lax.broadcasted_iota(jnp.int32, (MAXLEN, 1), 0)
    kind = lax.rem(b, 3)
    shift = 9 - kind
    seg = lax.shift_right_logical(pos, shift)
    off = pos - lax.shift_left(seg, shift)
    picked = jnp.full((MAXLEN, 1), len_ref[b, 0], jnp.int32)
    for slot in range(1, 4):
        picked = jnp.where(seg == slot, len_ref[b, slot], picked)
    return (off < picked).astype(F32)


def norm_stats(x):
    center = x - jnp.mean(x, axis=-1, keepdims=True)
    inverse = lax.rsqrt(jnp.mean(center * center, axis=-1, keepdims=True) + EPSILON)
    return center * inverse, inverse


def accumulate(ref, value, first_step):
    @pl.when(first_step)
    def _():
        ref[...] = value

    @pl.when(jnp.logical_not(first_step))
    def _():
        ref[...] += value


def ff_fwd_kernel(
    len_ref, h_ref, co_ref, cp_ref, cot_ref, wmo_ref, wmp_ref, wio_ref, wip_ref, woo_ref, wop_ref, vec_ref, pvec_ref,
    out_ref, x_ref, low_ref, gs_ref, lo_ref, gpo_ref, gpp_ref, owk_ref, owa_ref, sums_ref, act_ref, pa_ref, pb_ref,
):
    b = pl.program_id(0)
    d = h_ref.shape[1]
    ff = wio_ref.shape[1]
    width = 1536
    pa_ref[...] = dot(co_ref[...], wmo_ref[...])
    pb_ref[...] = dot(cp_ref[...], wmp_ref[...])
    mixed = (pa_ref[...] + pb_ref[...]) + vector(vec_ref, V_MB)
    x = h_ref[...].astype(F32) + mixed
    x_ref[...] = x
    n1, _ = norm_stats(x)
    first = n1 * vector(vec_ref, V_FG) + vector(vec_ref, V_FB)
    low = first.astype(BF)
    low_ref[...] = low
    for wi, wo, vec, gp_ref, part_ref, keep in (
        (wio_ref, woo_ref, vec_ref, gpo_ref, pa_ref, True),
        (wip_ref, wop_ref, pvec_ref, gpp_ref, pb_ref, False),
    ):
        part = None
        for c in range(ff // width):
            cols = slice(c * width, (c + 1) * width)
            inner = dot(low, wi[:, cols]) + vec[V_IB : V_IB + 1, cols]
            cdf = 0.5 * (1.0 + lax.erf(inner * INV_SQRT2))
            gp_ref[:, cols] = cdf + inner * (jnp.exp(-0.5 * inner * inner) * INV_SQRT_2PI)
            active = (inner * cdf).astype(BF)
            if keep:
                act_ref[:, cols] = active
            term = dot(active, wo[cols, :])
            part = term if part is None else part + term
        part_ref[...] = part
    r = first + ((pa_ref[...] + pb_ref[...]) + vector(vec_ref, V_OB))
    n2, inv2 = norm_stats(r)
    gain = vector(vec_ref, V_SG)
    out_ref[...] = (n2 * gain + vector(vec_ref, V_SB)).astype(BF)
    g = cot_ref[...].astype(F32) * live_column(len_ref, b)
    scaled = g * gain
    gs = inv2 * (
        scaled - jnp.mean(scaled, axis=-1, keepdims=True) - n2 * jnp.mean(scaled * n2, axis=-1, keepdims=True)
    )
    gs_ref[...] = gs
    lo = gs.astype(BF)
    lo_ref[...] = lo
    sums = jnp.concatenate(
        [
            jnp.sum(gs, axis=0, keepdims=True),
            jnp.sum(g * n2, axis=0, keepdims=True),
            jnp.sum(g, axis=0, keepdims=True),
            jnp.zeros((5, d), F32),
        ],
        axis=0,
    )
    accumulate(sums_ref, sums, b == 0)
    for ref, cols in zip((owk_ref, owa_ref), core_halves(ff // 2)):
        accumulate(ref, dot_at(act_ref[:, cols], lo), b == 0)


def ff_fwd(lengths, hidden, co, cp, cot, wmo, wmp, wio, wip, woo, wop, vec, pvec):
    n, d = hidden.shape
    half = co.shape[1]
    ff = wio.shape[1]
    return pl.pallas_call(
        ff_fwd_kernel,
        grid=(n // MAXLEN,),
        in_specs=[
            SMEM, rows_spec(d), rows_spec(half), rows_spec(half), rows_spec(d), full((half, d)), full((half, d)),
            full((d, ff)), full((d, ff)), full((ff, d)), full((ff, d)), full(vec.shape), full(pvec.shape),
        ],
        out_specs=[
            rows_spec(d), rows_spec(d), rows_spec(d), rows_spec(d), rows_spec(d), rows_spec(ff), rows_spec(ff),
            full((ff // 2, d)), full((ff // 2, d)), full((8, d)),
        ],
        out_shape=[
            jax.ShapeDtypeStruct((n, d), BF),
            jax.ShapeDtypeStruct((n, d), F32),
            jax.ShapeDtypeStruct((n, d), BF),
            jax.ShapeDtypeStruct((n, d), F32),
            jax.ShapeDtypeStruct((n, d), BF),
            jax.ShapeDtypeStruct((n, ff), F32),
            jax.ShapeDtypeStruct((n, ff), F32),
            jax.ShapeDtypeStruct((ff // 2, d), F32),
            jax.ShapeDtypeStruct((ff // 2, d), F32),
            jax.ShapeDtypeStruct((8, d), F32),
        ],
        scratch_shapes=[pltpu.VMEM((MAXLEN, ff), BF), pltpu.VMEM((MAXLEN, d), F32), pltpu.VMEM((MAXLEN, d), F32)],
        compiler_params=params(46),
        cost_estimate=cost(58),
        name="ff_fwd",
    )(lengths, hidden, co, cp, cot, wmo, wmp, wio, wip, woo, wop, vec, pvec)


def ff_bwd_half(lo, wi_ref, wo_ref, gp_ref, gi_ref, part_ref):
    width = 512
    part = None
    for c in range(wi_ref.shape[1] // width):
        cols = slice(c * width, (c + 1) * width)
        gi = (dot_bt(lo, wo_ref[cols, :]) * gp_ref[:, cols]).astype(BF)
        if gi_ref is not None:
            gi_ref[:, cols] = gi
        term = dot_bt(gi, wi_ref[:, cols])
        part = term if part is None else part + term
    part_ref[...] = part


def ff_bwd_own_kernel(skip, lo_ref, low_ref, gp_ref, wi_ref, wo_ref, *rest):
    part_ref, iwk_ref, iwa_ref, isum_ref, gi_ref = rest[skip:]
    b = pl.program_id(0)
    ff_bwd_half(lo_ref[...], wi_ref, wo_ref, gp_ref, gi_ref, part_ref)
    gi = gi_ref[...]
    for ref, cols in zip((iwk_ref, iwa_ref), core_halves(low_ref.shape[1] // 2)):
        accumulate(ref, dot_at(low_ref[:, cols], gi), b == 0)
    accumulate(isum_ref, jnp.sum(gi.astype(F32), axis=0, keepdims=True), b == 0)


def ff_bwd_own(lo, low, gp, wi, wo, *after):
    n, d = lo.shape
    ff = wi.shape[1]
    return pl.pallas_call(
        partial(ff_bwd_own_kernel, len(after)),
        grid=(n // MAXLEN,),
        in_specs=[rows_spec(d), rows_spec(d), rows_spec(ff), full((d, ff)), full((ff, d)), *[ANY] * len(after)],
        out_specs=[rows_spec(d), full((d // 2, ff)), full((d // 2, ff)), full((1, ff))],
        out_shape=[
            jax.ShapeDtypeStruct((n, d), F32),
            jax.ShapeDtypeStruct((d // 2, ff), F32),
            jax.ShapeDtypeStruct((d // 2, ff), F32),
            jax.ShapeDtypeStruct((1, ff), F32),
        ],
        scratch_shapes=[pltpu.VMEM((MAXLEN, ff), BF)],
        compiler_params=params(30),
        cost_estimate=cost(26),
        name="ff_bwd_own",
    )(lo, low, gp, wi, wo, *after)


def ff_bwd_peer_kernel(
    skip, lo_ref, gs_ref, x_ref, gp_ref, opart_ref, co_ref, wi_ref, wo_ref, vec_ref, *rest
):
    gm_ref, lm_ref, mwg_ref, sums_ref, part_ref = rest[skip:]
    b = pl.program_id(0)
    d = lo_ref.shape[1]
    ff_bwd_half(lo_ref[...], wi_ref, wo_ref, gp_ref, None, part_ref)
    g = gs_ref[...] + (opart_ref[...] + part_ref[...])
    n1, inv1 = norm_stats(x_ref[...])
    scaled = g * vector(vec_ref, V_FG)
    gm = inv1 * (
        scaled - jnp.mean(scaled, axis=-1, keepdims=True) - n1 * jnp.mean(scaled * n1, axis=-1, keepdims=True)
    )
    gm_ref[...] = gm
    lm = gm.astype(BF)
    lm_ref[...] = lm
    sums = jnp.concatenate(
        [
            jnp.sum(gm, axis=0, keepdims=True),
            jnp.sum(g * n1, axis=0, keepdims=True),
            jnp.sum(g, axis=0, keepdims=True),
            jnp.zeros((5, d), F32),
        ],
        axis=0,
    )
    accumulate(sums_ref, sums, b == 0)
    accumulate(mwg_ref, dot_at(co_ref[...], lm), b == 0)


def ff_bwd_peer(lo, gs, x, gp, opart, co, wi, wo, vec, *after):
    n, d = lo.shape
    half = co.shape[1]
    ff = wi.shape[1]
    return pl.pallas_call(
        partial(ff_bwd_peer_kernel, len(after)),
        grid=(n // MAXLEN,),
        in_specs=[
            rows_spec(d), rows_spec(d), rows_spec(d), rows_spec(ff), rows_spec(d), rows_spec(half), full((d, ff)),
            full((ff, d)), full(vec.shape), *[ANY] * len(after),
        ],
        out_specs=[rows_spec(d), rows_spec(d), full((half, d)), full((8, d))],
        out_shape=[
            jax.ShapeDtypeStruct((n, d), F32),
            jax.ShapeDtypeStruct((n, d), BF),
            jax.ShapeDtypeStruct((half, d), F32),
            jax.ShapeDtypeStruct((8, d), F32),
        ],
        scratch_shapes=[pltpu.VMEM((MAXLEN, d), F32)],
        compiler_params=params(30),
        cost_estimate=cost(25),
        name="ff_bwd_peer",
    )(lo, gs, x, gp, opart, co, wi, wo, vec, *after)


def attn_bwd_kernel(own, start, skip, len_ref, lm_ref, wm_ref, q_ref, k_ref, v_ref, l_ref, wq_ref, wk_ref, wv_ref, *rest):
    if own:
        given = 3 if start else 5
        h_ref, *given = rest[:given]
        part_ref, wk_out, wa_out, gc_ref, dq_ref, dk_ref, dv_ref = rest[len(given) + 1 + skip :]
    else:
        gm_ref, opart_ref = rest[:2]
        ig_ref, gc_ref, dq_ref, dk_ref, dv_ref, part_ref = rest[2 + skip :]
    half = wq_ref.shape[1]
    pairs = half // (2 * HD)
    b = pl.program_id(0) + start
    gc_ref[...] = dot_bt(lm_ref[...], wm_ref[...]).astype(BF)
    for kind in range(3):

        @pl.when(lax.rem(b, 3) == kind)
        def _():
            span = MAXLEN >> kind
            low_lanes = head_lanes(span)
            for seq in range(1 << kind):
                rows = slice(seq * span, (seq + 1) * span)
                live = lax.broadcasted_iota(jnp.int32, (span, 1), 0) < len_ref[b, seq]
                bias = jnp.where(live, 0.0, NEG)
                dqs, dks, dvs = [], [], []
                group = BWD_GROUP[kind]
                for first in range(0, 2 * pairs, group):
                    heads = range(first, first + group)
                    cols = [slice(head // 2 * 2 * HD, (head // 2 + 1) * 2 * HD) for head in heads]
                    masks = [low_lanes if head % 2 == 0 else ~low_lanes for head in heads]
                    qs = [q_ref[rows, at] * BF(0.125) for at in cols]
                    ups = [gc_ref[rows, at] for at in cols]
                    scores = [
                        dot_bt(k_ref[rows, at], jnp.where(mask, q, BF(0))) + bias for q, at, mask in zip(qs, cols, masks)
                    ]
                    dprobs = [
                        dot_bt(v_ref[rows, at], jnp.where(mask, up, BF(0))) for up, at, mask in zip(ups, cols, masks)
                    ]
                    probs = [jnp.exp(x - l_ref[head : head + 1, rows]) for x, head in zip(scores, heads)]
                    deltas = [jnp.sum(p * dp, axis=0, keepdims=True) for p, dp in zip(probs, dprobs)]
                    dscores = [(p * (dp - delta)).astype(BF) for p, dp, delta in zip(probs, dprobs, deltas)]
                    dvs += [dot(p.astype(BF), up) for p, up in zip(probs, ups)]
                    dks += [dot(ds, q) for ds, q in zip(dscores, qs)]
                    dqs += [dot_at(ds, k_ref[rows, at]) for ds, at in zip(dscores, cols)]
                for pair in range(pairs):
                    at = slice(pair * 2 * HD, (pair + 1) * 2 * HD)
                    dv_ref[rows, at] = jnp.where(low_lanes, dvs[2 * pair], dvs[2 * pair + 1]).astype(BF)
                    dk_ref[rows, at] = jnp.where(low_lanes, dks[2 * pair], dks[2 * pair + 1]).astype(BF)
                    dq = jnp.where(low_lanes, dqs[2 * pair], dqs[2 * pair + 1]) * 0.125
                    dq_ref[rows, at] = dq.astype(BF)

    dq, dk, dv = dq_ref[...], dk_ref[...], dv_ref[...]
    part = (dot_bt(dq, wq_ref[...]) + dot_bt(dk, wk_ref[...])) + dot_bt(dv, wv_ref[...])
    part_ref[...] = part
    if own:
        d = h_ref.shape[1]
        sums = jnp.concatenate(
            [jnp.sum(dq.astype(F32), axis=0, keepdims=True), jnp.sum(dv.astype(F32), axis=0, keepdims=True)], axis=1
        )
        first_step = b == start
        core = lax.axis_index("dp") & 1
        for side, (out, cols) in enumerate(zip((wk_out, wa_out), core_halves(half))):
            holds = (core == side).astype(F32)

            @pl.when(first_step)
            def _(side=side, out=out, cols=cols, holds=holds):
                if start:
                    out[...] = given[side][...]
                    return
                mwg_ref, fsum_ref, isum_ref, osum_ref = given
                pad = jnp.zeros((1, d), F32)
                top = jnp.concatenate([pad, fsum_ref[0:1, :]], axis=1)
                mid = jnp.concatenate([fsum_ref[1:2, :], fsum_ref[2:3, :]], axis=1)
                low = jnp.concatenate([osum_ref[0:1, :], osum_ref[1:2, :]], axis=1)
                end = jnp.concatenate([osum_ref[2:3, :], pad], axis=1)
                vectors = jnp.concatenate([top, mid, isum_ref[...], low, end, jnp.zeros((3, 2 * d), F32)], axis=0)
                out[:half, : 3 * half] = jnp.zeros((half, 3 * half), F32)
                out[:half, 3 * half :] = mwg_ref[:, cols]
                out[half : half + 8, :] = vectors * holds
                out[half + 8 :, :] = jnp.zeros((PAD - 8, 2 * d), F32)

            h = h_ref[:, cols]
            for i, grad in enumerate((dq, dk, dv)):
                out[:half, i * half : (i + 1) * half] += dot_at(h, grad)
            out[half : half + 1, :d] += sums * holds
    else:
        ig_ref[...] = (gm_ref[...] + (opart_ref[...] + part_ref[...])).astype(BF)


def attn_bwd(own, start, count, lengths, lm, wm, q, k, v, logs, wq, wk, wv, extra, prior=None, after=()):
    n, d = lm.shape
    half = wq.shape[1]
    after = ([] if prior is None else [prior]) + list(after)
    if own:
        extra_specs = [rows_spec(d, start)] + [full(x.shape) for x in extra[1:]]
        out_specs = [rows_spec(d, start)] + [full((half + PAD, 4 * half))] * 2
        out_shape = [jax.ShapeDtypeStruct((n, d), F32)] + [jax.ShapeDtypeStruct((half + PAD, 4 * half), F32)] * 2
    else:
        extra_specs = [rows_spec(d, start)] * 2
        out_specs = [rows_spec(d, start)]
        out_shape = [jax.ShapeDtypeStruct((n, d), BF)]
    return pl.pallas_call(
        partial(attn_bwd_kernel, own, start, len(after)),
        grid=(count,),
        in_specs=[
            SMEM, rows_spec(d, start), full((half, d)), rows_spec(half, start), rows_spec(half, start),
            rows_spec(half, start), pl.BlockSpec((8, MAXLEN), lambda b: (b + start, 0)), full((d, half)),
            full((d, half)), full((d, half)), *extra_specs, *[ANY] * len(after),
        ],
        out_specs=out_specs,
        out_shape=out_shape,
        input_output_aliases={} if prior is None else {10 + len(extra): 0},
        scratch_shapes=[pltpu.VMEM((MAXLEN, half), BF)] * 4 + ([] if own else [pltpu.VMEM((MAXLEN, d), F32)]),
        compiler_params=params(26 if own else 60),
        cost_estimate=cost(12 * count if own else 40),
        name="attn_bwd_own" if own else "attn_bwd_peer",
    )(lengths, lm, wm, q, k, v, logs, wq, wk, wv, *extra, *after)


CORE, NEAR, FAR = 1, 2, 4
TENSOR_SWAP = [(0, 1), (1, 0)]


def bit_of(mask):
    return (lax.axis_index("dp") & mask) != 0


def swap(x, mask, n_dp):
    return lax.ppermute(x, "dp", [(i, i ^ mask) for i in range(n_dp)])


def in_order(mask, mine, other):
    return jnp.where(bit_of(mask), jnp.concatenate([other, mine]), jnp.concatenate([mine, other]))


def away(x, mask):
    rows = x.shape[0] // 2
    return lax.dynamic_slice_in_dim(x, jnp.where(bit_of(mask), 0, rows), rows, 0)


def kept(x, mask):
    rows = x.shape[0] // 2
    return lax.dynamic_slice_in_dim(x, jnp.where(bit_of(mask), rows, 0), rows, 0)


def exchange(x, mask, n_dp):
    return swap(x, mask, n_dp) if mask < n_dp else jnp.zeros_like(x)


def join_kernel(mine_ref, other_ref, out_ref):
    rows = mine_ref.shape[0]
    core = lax.axis_index("dp") & 1
    out_ref[pl.ds(pl.multiple_of(core * rows, 8), rows), :] = mine_ref[...]
    out_ref[pl.ds(pl.multiple_of((1 - core) * rows, 8), rows), :] = other_ref[...]


def join(mine, other):
    return pl.pallas_call(
        join_kernel,
        out_shape=jax.ShapeDtypeStruct((2 * mine.shape[0], mine.shape[1]), mine.dtype),
        compiler_params=params(20),
        cost_estimate=cost(0.1),
        name="join",
    )(mine, other)


def beyond(x, n_dp):
    mask = 4 * FAR
    while mask < n_dp:
        x = x + swap(x, mask, n_dp)
        mask *= 2
    return x


def piece(arrays, masks, base, rows):
    index = jnp.int32(0)
    for mask in masks:
        index = index * 2 + bit_of(mask).astype(jnp.int32)
    cut = [lax.dynamic_slice_in_dim(a, base + index * rows, rows, 0) for a in arrays]
    return jnp.concatenate(cut, axis=1).astype(F32)


def tie(*arrays):
    return lax.optimization_barrier(arrays)


def prepare_kernel(*refs):
    weights, vectors, (vec_ref, out_ref) = refs[:4], refs[4:-2], refs[-2:]
    d = vec_ref.shape[1] // 2
    qb, vb, mb, fg, fb, ib, ob, sg, sb = [ref[...].astype(F32).reshape(1, -1) for ref in vectors]
    zero = jnp.zeros((1, d), F32)
    rows = [(qb, vb, mb), (fg, fb), (ib,), (ob, sg), (sb, zero)]
    vec = jnp.concatenate(
        [jnp.concatenate(row, axis=1) for row in rows] + [jnp.zeros((3, 2 * d), F32)], axis=0
    )
    vec_ref[...] = vec
    me = lax.axis_index("dp")
    core, near, far = me & 1, (me >> 1) & 1, (me >> 2) & 1
    half = d // 2
    rows = d // 16
    for base, index in ((0, core * 4 + far * 2 + near), (8 * rows, core * 4 + near * 2 + far)):
        at = pl.ds(pl.multiple_of(base + index * rows, 16), rows)
        to = slice(base // 8, base // 8 + rows)
        for i in range(3):
            out_ref[to, i * half : (i + 1) * half] = weights[i][at, :].astype(F32)
        at = pl.ds(pl.multiple_of(index * rows, 16), rows)
        cols = slice(0, half) if base == 0 else slice(half, d)
        out_ref[to, 3 * half :] = weights[3][at, cols].astype(F32)
    out_ref[2 * rows :, :] = vec


def prepare(weights, vectors):
    d = weights[0].shape[0]
    return pl.pallas_call(
        prepare_kernel,
        out_shape=[jax.ShapeDtypeStruct((8, 2 * d), F32), jax.ShapeDtypeStruct((d // 8 + 8, 2 * d), F32)],
        compiler_params=params(60),
        cost_estimate=cost(2),
        name="prepare",
    )(*weights, *vectors)


def finish_kernel(a_ref, ra_ref, b_ref, rb_ref, q_ref, k_ref, v_ref, m_ref, *vectors):
    half = m_ref.shape[0]
    d = 2 * half
    mine, other = core_halves(half)
    core = lax.axis_index("dp") & 1
    for cols, x_ref, y_ref in ((mine, a_ref, b_ref), (other, ra_ref, rb_ref)):
        q_ref[cols, :] = x_ref[:half, :half]
        k_ref[cols, :] = x_ref[:half, half:]
        v_ref[cols, :] = y_ref[:half, :half]
        m_ref[:, cols] = y_ref[:half, half:]
    pad = slice(half, half + 8)
    left = jnp.where(core == 0, a_ref[pad, :], ra_ref[pad, :])
    right = jnp.where(core == 0, b_ref[pad, :], rb_ref[pad, :])
    rows = (
        left[0:1, :half], left[0:1, half:], right[0:1], left[1:2], right[1:2],
        jnp.concatenate([left[2:3], right[2:3]], axis=1), left[3:4], right[3:4], left[4:5],
    )
    for ref, row in zip(vectors, rows):
        ref[...] = row.reshape(-1)


def finish(a, ra, b, rb):
    d = a.shape[1]
    half = d // 2
    return pl.pallas_call(
        finish_kernel,
        out_shape=[jax.ShapeDtypeStruct((d, half), F32)] * 3
        + [jax.ShapeDtypeStruct((half, d), F32)]
        + [jax.ShapeDtypeStruct((size,), F32) for size in (half, half, d, d, d, 2 * d, d, d, d)],
        compiler_params=params(20),
        cost_estimate=cost(0.1),
        name="finish",
    )(a, ra, b, rb)


def assemble_kernel(square, a_ref, ra_ref, b_ref, rb_ref, *outs):
    rows = a_ref.shape[0]
    odd = lax.axis_index("dp") & CORE
    for base, mine, other in ((0, a_ref, ra_ref), (2 * rows, b_ref, rb_ref)):
        for ref, side in ((mine, odd), (other, 1 - odd)):
            at = pl.ds(pl.multiple_of(base + side * rows, 16), rows)
            if not square:
                outs[0][at, :] = ref[...].astype(BF)
                continue
            half = ref.shape[1] // 4
            for i in range(3):
                outs[i][at, :] = ref[:, i * half : (i + 1) * half].astype(BF)
            at = pl.ds(pl.multiple_of(side * rows, 16), rows)
            left = base == 0
            cols = slice(0, half) if left else slice(half, 2 * half)
            outs[3][at, cols] = ref[:, 3 * half :].astype(BF)


def assemble(square, a, ra, b, rb):
    rows, cols = 4 * a.shape[0], a.shape[1]
    half = cols // 4
    if square:
        shapes = [(rows, half)] * 3 + [(rows // 2, 2 * half)]
    else:
        shapes = [(rows, cols)]
    return pl.pallas_call(
        partial(assemble_kernel, square),
        out_shape=[jax.ShapeDtypeStruct(shape, BF) for shape in shapes],
        compiler_params=params(16),
        cost_estimate=cost(4),
        name="assemble",
    )(a, ra, b, rb)


def local(
    n_dp, hidden_in, query_weight, key_weight, value_weight, query_bias, value_bias, mixer_weight, mixer_bias,
    first_gain, first_bias, inner_weight, inner_bias, outer_weight, outer_bias, second_gain, second_bias, lengths,
    cotangent,
):
    n, d = hidden_in.shape
    half = query_weight.shape[1]
    ff = inner_weight.shape[1]
    vec, h_out = prepare(
        (query_weight, key_weight, value_weight, mixer_weight),
        (
            query_bias, value_bias, mixer_bias, first_gain, first_bias, inner_bias, outer_bias, second_gain,
            second_bias,
        ),
    )
    sixteenth = d // 16
    i_out = jnp.concatenate(
        [
            piece([inner_weight], (CORE, FAR, NEAR), 0, sixteenth),
            piece([inner_weight], (CORE, NEAR, FAR), d // 2, sixteenth),
        ]
    )
    eighth = ff // 8
    o_out = jnp.concatenate(
        [piece([outer_weight], (CORE, NEAR), 0, eighth), piece([outer_weight], (CORE, FAR), ff // 2, eighth)]
    )
    h0 = lax.ppermute(h_out, "tensor", TENSOR_SWAP)
    own = list(attn_fwd(lengths, hidden_in, query_weight, key_weight, value_weight, vec, 0, 2))
    h0, i_out, own[0] = tie(h0, i_out, own[0])
    i0 = lax.ppermute(i_out, "tensor", TENSOR_SWAP)
    ha, hb, pvec = h0[:sixteenth], h0[sixteenth : 2 * sixteenth], h0[2 * sixteenth :]
    hra, hrb = swap(ha, NEAR, n_dp), swap(hb, FAR, n_dp)
    qo, ko, vo, co, lgo = attn_fwd(
        lengths, hidden_in, query_weight, key_weight, value_weight, vec, 2, 2, own, (ha, hb)
    )
    hra, hrb, i0, co, o_out = tie(hra, hrb, i0, co, o_out)
    ha, hb = in_order(NEAR, ha, hra), in_order(FAR, hb, hrb)
    hra, hrb = swap(ha, FAR, n_dp), swap(hb, NEAR, n_dp)
    o0 = lax.ppermute(o_out, "tensor", TENSOR_SWAP)
    ia, ib = i0[:sixteenth], i0[sixteenth:]
    ira, irb = swap(ia, NEAR, n_dp), swap(ib, FAR, n_dp)
    ha, hb = in_order(FAR, ha, hra), in_order(NEAR, hb, hrb)
    hra, hrb = swap(ha, CORE, n_dp), swap(hb, CORE, n_dp)
    ha, hb, ira, irb = tie(ha, hb, ira, irb)
    ia, ib = in_order(NEAR, ia, ira), in_order(FAR, ib, irb)
    ira, irb = swap(ia, FAR, n_dp), swap(ib, NEAR, n_dp)
    wqp, wkp, wvp, wmp = assemble(True, ha, hra, hb, hrb)
    peer = list(attn_fwd(lengths, hidden_in, wqp, wkp, wvp, pvec, 0, 2, None, (ia, ib), True))
    ira, irb, o0, peer[0] = tie(ira, irb, o0, peer[0])
    ia, ib = in_order(FAR, ia, ira), in_order(NEAR, ib, irb)
    ira, irb = swap(ia, CORE, n_dp), swap(ib, CORE, n_dp)
    oa, ob = o0[:eighth], o0[eighth:]
    ora, orb = swap(oa, NEAR, n_dp), swap(ob, FAR, n_dp)
    qp, kp, vp, cp, lgp = attn_fwd(lengths, hidden_in, wqp, wkp, wvp, pvec, 2, 2, peer, (ia, ib, oa, ob), True)
    ora, orb, cp = tie(ora, orb, cp)
    oa, ob = in_order(NEAR, oa, ora), in_order(FAR, ob, orb)
    ora, orb = swap(oa, CORE, n_dp), swap(ob, CORE, n_dp)
    (wip,) = assemble(False, ia, ira, ib, irb)
    (wop,) = assemble(False, oa, ora, ob, orb)
    layer_out, x, low, gs, lo, gpo, gpp, owk, owa, osums = ff_fwd(
        lengths, hidden_in, co, cp, cotangent, mixer_weight, wmp, inner_weight, wip, outer_weight, wop, vec, pvec
    )
    o, lo = tie(swap(owa, CORE, n_dp), lo)
    o1 = owk + o
    o_out = away(o1, NEAR)
    o = swap(o_out, NEAR, n_dp)
    opart, iwk, iwa, ibg = ff_bwd_own(lo, low, gpo, inner_weight, outer_weight, o_out)
    o, opart, iwa = tie(o, opart, iwa)
    i, opart = tie(swap(iwa, CORE, n_dp), opart)
    i1 = iwk + i
    i_out = away(i1, NEAR)
    i = swap(i_out, NEAR, n_dp)
    o2 = kept(o1, NEAR) + o
    o_out = away(o2, FAR)
    o = swap(o_out, FAR, n_dp)
    gm, lm, mwg, isums = ff_bwd_peer(lo, gs, x, gpp, opart, co, wip, wop, vec, o_out, i_out)
    o, i, lm = tie(o, i, lm)
    i2 = kept(i1, NEAR) + i
    i_out = away(i2, FAR)
    o3 = kept(o2, FAR) + o
    o = exchange(o3, 2 * FAR, n_dp)
    i_out, o3 = tie(i_out, o3)
    i = swap(i_out, FAR, n_dp)
    own = (lengths, lm, mixer_weight, qo, ko, vo, lgo, query_weight, key_weight, value_weight)
    part, hk, ha = attn_bwd(True, 0, 2, *own, (hidden_in, mwg, isums, ibg, osums), None, (o3, i_out))
    o, i, part = tie(o, i, part)
    o = beyond(o3 + o, n_dp)
    o_ = swap(o, FAR, n_dp)
    i3 = kept(i2, FAR) + i
    i3, o = tie(i3, o)
    i = exchange(i3, 2 * FAR, n_dp)
    part, hk, ha = attn_bwd(True, 2, 2, *own, (hidden_in, hk, ha), part, (o, i3))
    h = swap(ha, CORE, n_dp)
    o_, ha = tie(o_, ha)
    o = in_order(FAR, o, o_)
    cut = o.shape[0] // 2
    oa_, ob = swap(o[:cut], NEAR, n_dp), o[cut:]
    peer = (lengths, lm, wmp, qp, kp, vp, lgp, wqp, wkp, wvp)
    (ig,) = attn_bwd(False, 1, 1, *peer, (gm, part), None, (o,))
    h, i, ig = tie(h, i, ig)
    h1 = hk + h
    ha, hb = h1[:, :d], h1[:, d:]
    ha_out, hb_out = away(ha, NEAR), away(hb, FAR)
    hra, hrb = swap(ha_out, NEAR, n_dp), swap(hb_out, FAR, n_dp)
    i = beyond(i3 + i, n_dp)
    i, hb_out = tie(i, hb_out)
    i_ = swap(i, FAR, n_dp)
    (ig,) = attn_bwd(False, 0, 1, *peer, (gm, part), ig, (ha_out, hb_out, i))
    hra, hrb, ob, ig = tie(hra, hrb, ob, ig)
    ha, hb = kept(ha, NEAR) + hra, kept(hb, FAR) + hrb
    ha_out, hb_out = away(ha, FAR), away(hb, NEAR)
    hra, hrb = swap(ha_out, FAR, n_dp), swap(hb_out, NEAR, n_dp)
    ob, hb_out = tie(ob, hb_out)
    ob_ = swap(ob, NEAR, n_dp)
    (ig,) = attn_bwd(False, 2, 1, *peer, (gm, part), ig, (ha_out, hb_out, ob))
    hra, hrb, i_, ig = tie(hra, hrb, i_, ig)
    h = jnp.concatenate([kept(ha, FAR) + hra, kept(hb, NEAR) + hrb])
    h_ = exchange(h, 2 * FAR, n_dp)
    i = in_order(FAR, i, i_)
    i_ = swap(i, NEAR, n_dp)
    (input_grad,) = attn_bwd(False, 3, 1, *peer, (gm, part), ig, (h, i))
    h_, input_grad = tie(h_, input_grad)
    h = beyond(h + h_, n_dp)
    rows = h.shape[0] // 2
    ha, hb = h[:rows], h[rows:]
    hra, hrb = swap(ha, FAR, n_dp), swap(hb, NEAR, n_dp)
    hra, hrb, i_, oa_, ob_ = tie(hra, hrb, i_, oa_, ob_)
    ha, hb = in_order(FAR, ha, hra), in_order(NEAR, hb, hrb)
    hra, hrb = swap(ha, NEAR, n_dp), swap(hb, FAR, n_dp)
    i = in_order(NEAR, i, i_)
    i_ = swap(i, CORE, n_dp)
    o = in_order(NEAR, o, jnp.concatenate([oa_, ob_]))
    o_ = swap(o, CORE, n_dp)
    owg = join(o, o_)
    hra, hrb, owg, i_ = tie(hra, hrb, owg, i_)
    ha, hb = in_order(NEAR, ha, hra), in_order(FAR, hb, hrb)
    hra, hrb = swap(ha, CORE, n_dp), swap(hb, CORE, n_dp)
    iwg = join(i, i_)
    hra, hrb, iwg = tie(hra, hrb, iwg)
    qwg, kwg, vwg, mwg, *vectors = finish(ha, hra, hb, hrb)
    qb, vb, mb, fg, fb, ib, ob, sg, sb = vectors
    return (
        layer_out, input_grad, qwg, kwg, vwg, qb, vb, mwg, mb, fg, fb, iwg, ib, owg, ob, sg, sb,
    )


def solution(mesh):
    col, row, rep = P(None, "tensor"), P("tensor", None), P()
    vec, tok = P("tensor"), P("dp", None)
    return jax.shard_map(
        partial(local, mesh.shape["dp"]),
        mesh=mesh,
        in_specs=(tok, col, col, col, vec, vec, row, rep, rep, rep, col, vec, row, rep, rep, rep, tok, tok),
        out_specs=(tok, tok, col, col, col, vec, vec, row, rep, rep, rep, col, vec, row, rep, rep, rep),
        check_vma=False,
    )
```
